128 devices in a mesh: gx: 8 (over x, core), gy: 16 (over z, y).
Axes of the slice: x: 4, y: 4, z: 4, core: 2. Of those that a mesh axis runs over, the one named last changes fastest.
Arguments:
- latents: bfloat16 [8, 16, 24, 512, 128], P('gx', 'gy'), may hold values from -6 to 6
- gain_first: float32 [128], replicated, may hold values from 0.5 to 1.5
- conv_first: bfloat16 [7, 128, 128], replicated, may hold values from -0.1875 to 0.1875
- gain_second: float32 [128], replicated, may hold values from 0.5 to 1.5
- conv_second: bfloat16 [7, 128, 128], replicated, may hold values from -0.1875 to 0.1875
- upward: bfloat16 [2, 2, 2, 128, 128], replicated, may hold values from -0.5 to 0.5
- neighbour_owner: int32 [8, 16, 24, 6], P('gx', 'gy'), may hold values from -1 to 127, as said below
- neighbour_slot: int32 [8, 16, 24, 6], P('gx', 'gy'), may hold values from -1 to 23, as said below
- destination_device: int32 [8, 16, 24], P('gx', 'gy'), may hold values from -1 to 15, as said below
- destination_slot: int32 [8, 16, 24], P('gx', 'gy'), may hold values from -1 to 23, as said below
Outputs:
- children: bfloat16 [8, 16, 192, 512, 128], P('gx', 'gy')
The draws below stay inside these ranges and needn't reach their ends.
Inputs may be any that keep to these rules, and one draw needn't show every extreme that they name: `neighbour_owner`: -1 where the slot is empty or the face has no active neighbour. Across an x face the owner is this device or the adjacent device along gx on that side, across a y face this device or the adjacent device along gy on that side, across a z face this device; faces on the grid's outer boundary have no neighbour. Neighbourhood is symmetric and agrees with neighbour_slot. `neighbour_slot`: -1 exactly where neighbour_owner is -1; else an occupied slot of the owner. `destination_device`: -1 for empty slots; the occupied slots of a device are its first ones. In each gx group the occupied blocks, taken in order of gy index and slot, go to the group's devices in turn from some starting device, so at most 2 blocks go from one device to one destination. `destination_slot`: -1 for empty slots; for the r-th occupied block of a gx group (counted from 0) it is r // 16; occupied blocks of a group have distinct destinations and slots.
All inputs are finite; a program needn't handle non-finite values.
Results may differ from the reference program's by a relative error of at most 0.0054.
Values may be sent and summed in bfloat16 or wider, within the bound.
A program may use at most 256 MiB of HBM per device.

```python
import jax
import jax.numpy as jnp
from jax import lax

C = 128
E = 8
P_SIZE = 24
N_GX = 8
N_GY = 16


def block_layout(key):
    depth = P_SIZE // 2
    spots = 2 * P_SIZE
    keys = jax.random.split(key, 4)
    grade = jax.random.randint(keys[0], (N_GX, N_GY), 0, 17)
    counts_live = P_SIZE // 2 + (P_SIZE - P_SIZE // 2) * grade * grade // 256
    chosen = jax.random.randint(keys[1], (), 0, N_GX)
    row_ids = jnp.broadcast_to(jnp.arange(N_GX, dtype=jnp.int32)[:, None], (N_GX, N_GY))
    counts_live = jnp.where(row_ids == chosen, P_SIZE, counts_live).astype(jnp.int32)
    scores = jax.random.randint(keys[2], (N_GX, N_GY, spots), 0, 2 ** 20) * spots + jnp.arange(spots, dtype=jnp.int32)
    ranking = jnp.argsort(jnp.argsort(scores, axis=-1, stable=True), axis=-1, stable=True)
    is_live = ranking < counts_live[:, :, None]
    slot_at = jnp.where(is_live, jnp.cumsum(is_live.astype(jnp.int32), axis=-1) - 1, -1).astype(jnp.int32)
    grid_slot = slot_at.reshape(N_GX, N_GY, 2, 2, depth).transpose(0, 2, 1, 3, 4).reshape(2 * N_GX, 2 * N_GY, depth)
    owner_grid = (jnp.arange(2 * N_GX, dtype=jnp.int32) // 2)[:, None, None] * N_GY + (jnp.arange(2 * N_GY, dtype=jnp.int32) // 2)[None, :, None]
    owner_grid = jnp.broadcast_to(owner_grid, grid_slot.shape)
    owner_grid = jnp.where(grid_slot >= 0, owner_grid, -1)
    padded_slot = jnp.pad(grid_slot, 1, constant_values=-1)
    padded_owner = jnp.pad(owner_grid, 1, constant_values=-1)

    def beside_all(padded):
        return jnp.stack([padded[2:, 1:-1, 1:-1], padded[:-2, 1:-1, 1:-1], padded[1:-1, 2:, 1:-1], padded[1:-1, :-2, 1:-1], padded[1:-1, 1:-1, 2:], padded[1:-1, 1:-1, :-2]], axis=-1)

    def to_devices(grid):
        return grid.reshape(N_GX, 2, N_GY, 2, depth, 6).transpose(0, 2, 1, 3, 4, 5).reshape(N_GX, N_GY, spots, 6)
    near_slot = to_devices(beside_all(padded_slot))
    near_owner = to_devices(beside_all(padded_owner))
    matches = slot_at[:, :, None, :] == jnp.arange(P_SIZE, dtype=jnp.int32)[None, None, :, None]
    filled = jnp.any(matches, axis=-1)[..., None]
    table_slot = jnp.sum(matches[..., None].astype(jnp.int32) * near_slot[:, :, None], axis=3)
    table_owner = jnp.sum(matches[..., None].astype(jnp.int32) * near_owner[:, :, None], axis=3)
    table_slot = jnp.where(filled, table_slot, -1).astype(jnp.int32)
    table_owner = jnp.where(filled, table_owner, -1).astype(jnp.int32)
    table_owner = jnp.where(table_slot >= 0, table_owner, -1).astype(jnp.int32)
    before = jnp.cumsum(counts_live, axis=1) - counts_live
    order = before[:, :, None] + jnp.arange(P_SIZE, dtype=jnp.int32)[None, None, :]
    start = jax.random.randint(keys[3], (N_GX, 1, 1), 0, N_GY)
    live_slot = jnp.arange(P_SIZE, dtype=jnp.int32)[None, None, :] < counts_live[:, :, None]
    dest_dev = jnp.where(live_slot, (order + start) % N_GY, -1).astype(jnp.int32)
    dest_slot = jnp.where(live_slot, order // N_GY, -1).astype(jnp.int32)
    return (table_owner, table_slot, dest_dev, dest_slot)


def draw_neighbour_owner(key, part):
    shared = block_layout(key)
    return shared[0]


def draw_neighbour_slot(key, part):
    shared = block_layout(key)
    return shared[1]


def draw_destination_device(key, part):
    shared = block_layout(key)
    return shared[2]


def draw_destination_slot(key, part):
    shared = block_layout(key)
    return shared[3]


def level_of(key, extent, cuts, least, top_value):
    loudness = 1.0
    for position, parts in cuts:
        heights = jax.random.uniform(jax.random.fold_in(jax.random.fold_in(key, 6), position), (parts,), jnp.float32, least / len(cuts), top_value / len(cuts))
        loudness = loudness * jnp.repeat(jnp.exp(heights), extent[position] // parts).reshape((-1,) + (1,) * (len(extent) - 1 - position))
    return loudness


def centred(own_key, dims, width, most, pieces=(), held_as=jnp.bfloat16):
    level = level_of(own_key, dims, pieces, -0.22, 0.18) if pieces else 1.0
    entries = jax.random.normal(own_key, dims, jnp.float32) * width * level
    return jnp.minimum(jnp.maximum(entries, -most), most).astype(held_as)


def setup_inputs(seed: int = 0) -> dict:
    key_of = jax.random.split(jax.random.key(seed), 11)
    latents = centred(key_of[0], (N_GX, N_GY, P_SIZE, E**3, C), 1.0, 6.0, ((0, 8), (1, 16)))
    gain_first = jnp.clip(jax.random.uniform(key_of[1], (C,), jnp.float32, 0.5, 1.5), 0.5, 1.5)
    conv_first = centred(key_of[2], (7, C, C), (7 * C) ** -0.5, 0.1875)
    gain_second = jnp.clip(jax.random.uniform(key_of[3], (C,), jnp.float32, 0.5, 1.5), 0.5, 1.5)
    conv_second = centred(key_of[4], (7, C, C), (7 * C) ** -0.5, 0.1875)
    upward = centred(key_of[5], (2, 2, 2, C, C), C ** -0.5, 0.5)
    neighbour_owner = draw_neighbour_owner(jax.random.fold_in(key_of[10], 71), 0)
    neighbour_slot = draw_neighbour_slot(jax.random.fold_in(key_of[10], 71), 0)
    destination_device = draw_destination_device(jax.random.fold_in(key_of[10], 71), 0)
    destination_slot = draw_destination_slot(jax.random.fold_in(key_of[10], 71), 0)
    return dict(latents=latents, gain_first=gain_first, conv_first=conv_first, gain_second=gain_second, conv_second=conv_second, upward=upward, neighbour_owner=neighbour_owner, neighbour_slot=neighbour_slot, destination_device=destination_device, destination_slot=destination_slot)


def normed(values, gain_vec):
    floats = values.astype(jnp.float32)
    scale = lax.rsqrt(lax.optimization_barrier(jnp.mean(floats * floats, axis=-1, keepdims=True)) + 1e-06)
    return jax.nn.silu(floats * scale * gain_vec).astype(jnp.bfloat16)

def taps(active, face_list, kernel):
    count_blocks = active.shape[0]
    edge = active.shape[1]
    channels = active.shape[-1]
    stacked = kernel.transpose(1, 0, 2).reshape(channels, 7 * channels)
    whole = jnp.dot(active.reshape(-1, channels), stacked, preferred_element_type=jnp.float32)
    whole = whole.reshape(count_blocks, edge, edge, edge, 7 * channels)
    summed = whole[..., :channels]
    for face_index in range(6):
        tap_index = face_index + 1
        part = whole[..., tap_index * channels:(tap_index + 1) * channels]
        face_term = jnp.dot(face_list[face_index].reshape(-1, channels), kernel[tap_index], preferred_element_type=jnp.float32)
        face_term = face_term.reshape(face_list[face_index].shape)
        axis = 1 + face_index // 2
        face_term = jnp.expand_dims(face_term, axis)
        if face_index % 2 == 0:
            inner = lax.slice_in_dim(part, 1, edge, axis=axis)
            shifted = jnp.concatenate([inner, face_term], axis=axis)
        else:
            inner = lax.slice_in_dim(part, 0, edge - 1, axis=axis)
            shifted = jnp.concatenate([face_term, inner], axis=axis)
        summed = summed + shifted
    return summed.reshape(-1, channels)

def subdivide(blocks, upward):
    count_blocks = blocks.shape[0]
    channels = blocks.shape[-1]
    half = E // 2
    upward_mat = upward.transpose(3, 0, 1, 2, 4).reshape(channels, 8 * channels)
    product = jnp.dot(blocks.reshape(-1, channels), upward_mat, preferred_element_type=jnp.float32).astype(jnp.bfloat16)
    product = product.reshape(count_blocks, 2, half, 2, half, 2, half, 2, 2, 2, channels)
    product = product.transpose(0, 1, 3, 5, 2, 7, 4, 8, 6, 9, 10)
    return product.reshape(count_blocks, 8, E ** 3, channels)

def convolve_all(active, owners, slot_ids, kernel):
    block_total = active.shape[0]
    layers = [active[:, 0], active[:, -1], active[:, :, 0], active[:, :, -1], active[:, :, :, 0], active[:, :, :, -1]]
    face_list = []
    for face_index in range(6):
        target = owners[:, face_index] * P_SIZE + slot_ids[:, face_index]
        picked = jnp.take(layers[face_index], jnp.clip(target, 0, block_total - 1), axis=0)
        valid = (slot_ids[:, face_index] >= 0)[:, None, None, None]
        face_list.append(jnp.where(valid, picked, jnp.zeros_like(picked)))
    grouped = active.reshape(N_GX, N_GY * P_SIZE, E, E, E, C)
    grouped_faces = tuple((item.reshape(N_GX, N_GY * P_SIZE, E, E, C) for item in face_list))

    def one_group(group_pair):
        return taps(group_pair[0], list(group_pair[1]), kernel)
    result = lax.map(one_group, (grouped, grouped_faces))
    return result.reshape(-1, C)

def reference(latents, gain_first, conv_first, gain_second, conv_second, upward, neighbour_owner, neighbour_slot, destination_device, destination_slot):
    block_total = N_GX * N_GY * P_SIZE
    blocks = latents.reshape(block_total, E, E, E, C)
    owners = neighbour_owner.reshape(block_total, 6)
    slot_ids = neighbour_slot.reshape(block_total, 6)
    first = normed(blocks, gain_first)
    mixed = convolve_all(first, owners, slot_ids, conv_first)
    second = normed(mixed.reshape(block_total, E, E, E, C), gain_second)
    branch = convolve_all(second, owners, slot_ids, conv_second)
    hidden = (blocks.reshape(block_total * E ** 3, C).astype(jnp.float32) + branch).astype(jnp.bfloat16)
    hidden = hidden.reshape(block_total, E ** 3, C)
    column = N_GY * P_SIZE
    dest_dev = destination_device.reshape(N_GX, column)
    dest_slot = destination_slot.reshape(N_GX, column)
    target = jnp.where(dest_dev >= 0, dest_dev * P_SIZE + dest_slot, column).astype(jnp.int32)
    row_ids = jnp.broadcast_to(jnp.arange(N_GX, dtype=jnp.int32)[:, None], (N_GX, column))
    source_ids = jnp.broadcast_to(jnp.arange(column, dtype=jnp.int32)[None, :], (N_GX, column))
    sources = jnp.full((N_GX, column), -1, jnp.int32).at[row_ids, target].set(source_ids, mode='drop')
    global_src = row_ids * column + sources
    moved = jnp.take(hidden, jnp.clip(global_src, 0, block_total - 1).reshape(-1), axis=0)
    moved = jnp.where((sources >= 0).reshape(-1)[:, None, None], moved, jnp.zeros_like(moved))
    children = lax.map(lambda grouped: subdivide(grouped, upward), moved.reshape(N_GX, column, E ** 3, C))
    return children.reshape(N_GX, N_GY, 8 * P_SIZE, E ** 3, C)
```

```python
import jax
import jax.numpy as jnp
from jax import lax
from jax.experimental import pallas as pl
from jax.experimental.pallas import tpu as pltpu
from jax.sharding import PartitionSpec as P

MESH = pl.DeviceIdType.MESH
BF = jnp.bfloat16
F32 = jnp.float32
S = 24
C = 128
CELLS = 512
LAYER = 64
GROUPS = 4
GS = S // GROUPS
CHUNKS = 4
CR = CELLS // CHUNKS
LIMIT = 60 * 2**20


def dot(a, b):
    return jnp.dot(a, b, preferred_element_type=F32)


def silu_norm(m, half_gain):
    scale = lax.rsqrt(jnp.mean(m * m, axis=-1, keepdims=True) + 1e-6)
    h = m * scale * half_gain
    return (h + h * jnp.tanh(h)).astype(BF)


def branch_kernel(
    lat, g1, k1, g2, k2, owner, slot, dest, out,
    first, second, yl1, yh1, yl2, yh2,
    ra0, ra1, ra2, ra3, rb0, rb1, rb2, rb3,
    mixed, weights, send_sem, recv_sem,
):
    gx = lax.axis_index("gx")
    gy = lax.axis_index("gy")
    n_gx = lax.axis_size("gx")
    n_gy = lax.axis_size("gy")
    me = gx * n_gy + gy
    west = (lax.rem(gx + n_gx - 1, n_gx), gy)
    east = (lax.rem(gx + 1, n_gx), gy)
    south = (gx, lax.rem(gy + n_gy - 1, n_gy))
    north = (gx, lax.rem(gy + 1, n_gy))
    targets = (west, east, south, north)

    barrier = pltpu.get_barrier_semaphore()
    for t in targets:
        pl.semaphore_signal(barrier, inc=1, device_id=t, device_id_type=MESH)

    zero = jnp.zeros((LAYER, C), BF)
    for buf in (yl1, yh1, yl2, yh2, ra0, ra1, ra2, ra3, rb0, rb1, rb2, rb3):
        buf[S] = zero
    for buf in (first, second):
        for q in range(8):
            buf[S, q * LAYER : (q + 1) * LAYER] = zero

    recv = ((ra0, ra1, ra2, ra3), (rb0, rb1, rb2, rb3))
    acts = (first, second)
    y_lo = (yl1, yl2)
    y_hi = (yh1, yh2)
    gains = (g1, g2)
    taps = (k1, k2)

    def copies(n, g):
        blocks = pl.ds(g * GS, GS)
        src = (
            acts[n].at[blocks, pl.ds(0, LAYER)],
            acts[n].at[blocks, pl.ds(CELLS - LAYER, LAYER)],
            y_lo[n].at[blocks],
            y_hi[n].at[blocks],
        )
        return [
            pltpu.make_async_remote_copy(
                src_ref=src[i],
                dst_ref=recv[n][i].at[blocks],
                send_sem=send_sem.at[n, i, g],
                recv_sem=recv_sem.at[n, i, g],
                device_id=targets[i],
                device_id_type=MESH,
            )
            for i in range(4)
        ]

    def emit(n, b, q, m):
        act = silu_norm(m, gains[n][...] * 0.5)
        acts[n][b, q * 128 : (q + 1) * 128] = act
        return act

    def emit_y(n, b, q, m, half_gain):
        h0 = silu_norm_f32(m, half_gain)
        acts[n][b, q * 128 : (q + 1) * 128] = h0.astype(BF)
        y_lo[n][b, q * 16 : (q + 1) * 16] = jnp.concatenate([h0[0:8], h0[64:72]], 0).astype(BF)
        y_hi[n][b, q * 16 : (q + 1) * 16] = jnp.concatenate([h0[56:64], h0[120:128]], 0).astype(BF)

    def silu_norm_f32(m, half_gain):
        scale = lax.rsqrt(jnp.mean(m * m, axis=-1, keepdims=True) + 1e-6)
        h = m * scale * half_gain
        return h + h * jnp.tanh(h)

    def local_slot(b, f):
        s = slot[b, f]
        return jnp.where((s >= 0) & (owner[b, f] == me), s, S)

    def remote_slot(b, f):
        s = slot[b, f]
        return jnp.where((s >= 0) & (owner[b, f] != me), s, S)

    half_1 = g1[...] * 0.5

    def norm_group(g, carry):
        def one(b, carry):
            for q in range(4):
                emit_y(0, b, q, lat[b, q * 128 : (q + 1) * 128].astype(F32), half_1)
            return carry

        lax.fori_loop(g * GS, (g + 1) * GS, one, 0)
        for c in copies(0, g):
            c.start()
        return carry

    pl.semaphore_wait(barrier, 4)
    lax.fori_loop(0, GROUPS, norm_group, 0)

    for n in range(2):
        k = taps[n]
        z = jnp.zeros((C, C), BF)
        tiles = (
            ((k[0], k[3]), (k[1], z)),
            ((z, k[4]), (k[2], z)),
            ((k[5], z), (z, k[6])),
            ((k[1], z), (z, k[2])),
            ((k[3], z), (z, k[4])),
        )
        for w in range(5):
            for r in range(2):
                for c in range(2):
                    weights[n, w, r * C : (r + 1) * C, c * C : (c + 1) * C] = tiles[w][r][c]

    row = lax.broadcasted_iota(jnp.int32, (128, C), 0) % 8
    low = jnp.where(row == 0, 1.0, 0.0).astype(BF)
    not_low = jnp.where(row == 0, 0.0, 1.0).astype(BF)
    high = jnp.where(row == 7, 1.0, 0.0).astype(BF)
    not_high = jnp.where(row == 7, 0.0, 1.0).astype(BF)

    def inner(n, b):
        v = acts[n]
        up = local_slot(b, 4)
        down = local_slot(b, 5)
        zero8 = jnp.zeros((8, C), F32)
        for q in range(4):
            lo, hi = q * 128, (q + 1) * 128
            here = v[b, lo:hi]
            after = v[b, lo + 64 : hi + 64] if q < 3 else jnp.concatenate([v[b, lo + 64 : hi], zero], 0)
            before = v[b, lo - 64 : hi - 64] if q > 0 else jnp.concatenate([zero, v[b, lo : hi - 64]], 0)
            a = dot(jnp.concatenate([here, after], 1), weights[n, 0])
            p = dot(jnp.concatenate([here, before], 1), weights[n, 1])
            z_up = here * not_low + v[up, lo:hi] * low
            z_down = here * not_high + v[down, lo:hi] * high
            z = dot(jnp.concatenate([z_up, z_down], 1), weights[n, 2])
            total = a[:, :C] + p[:, :C]
            total += pltpu.roll(z[:, :C].reshape(16, 8, C), 7, 1).reshape(128, C)
            total += pltpu.roll(z[:, C:].reshape(16, 8, C), 1, 1).reshape(128, C)
            yp, ym = a[:, C:], p[:, C:]
            total += jnp.concatenate([yp[8:64], zero8, yp[72:128], zero8], 0)
            total += jnp.concatenate([zero8, ym[0:56], zero8, ym[64:120]], 0)
            mixed[b, lo:hi] = total

    def faces(n, b):
        v, r = acts[n], recv[n]
        x_pair = jnp.concatenate(
            [
                v[local_slot(b, 0), 0:LAYER] + r[0][remote_slot(b, 0)],
                v[local_slot(b, 1), CELLS - LAYER : CELLS] + r[1][remote_slot(b, 1)],
            ],
            1,
        )
        y_pair = jnp.concatenate(
            [
                y_lo[n][local_slot(b, 2)] + r[2][remote_slot(b, 2)],
                y_hi[n][local_slot(b, 3)] + r[3][remote_slot(b, 3)],
            ],
            1,
        )
        return dot(x_pair, weights[n, 3]), dot(y_pair, weights[n, 4])

    def whole(b, q, fx, fy):
        m = mixed[b, q * 128 : (q + 1) * 128]
        lo, hi = fy[q * 16 : (q + 1) * 16, C:], fy[q * 16 : (q + 1) * 16, :C]
        m0, m1 = m[0:64], m[64:128]
        if q == 0:
            m0 = m0 + fx[:, C:]
        if q == 3:
            m1 = m1 + fx[:, :C]
        return jnp.concatenate(
            [
                m0[0:8] + lo[0:8], m0[8:56], m0[56:64] + hi[0:8],
                m1[0:8] + lo[8:16], m1[8:56], m1[56:64] + hi[8:16],
            ],
            0,
        )

    def run_inner(n):
        def one(b, carry):
            inner(n, b)
            return carry

        lax.fori_loop(0, S, one, 0)

    def wait_faces(n):
        def one(g, carry):
            for c in copies(n, g):
                c.wait_recv()
            return carry

        lax.fori_loop(0, GROUPS, one, 0)

    run_inner(0)
    wait_faces(0)

    half_2 = g2[...] * 0.5

    def second_group(g, carry):
        def one(b, carry):
            fx, fy = faces(0, b)
            for q in range(4):
                emit_y(1, b, q, whole(b, q, fx, fy), half_2)
            return carry

        lax.fori_loop(g * GS, (g + 1) * GS, one, 0)
        for c in copies(1, g):
            c.start()
        return carry

    lax.fori_loop(0, GROUPS, second_group, 0)
    run_inner(1)
    wait_faces(1)

    base = dest[0, 0]

    def hidden_one(p, carry):
        y = gy + p // 6
        b = ((y - base) & 3) + 4 * (p % 6)
        fx, fy = faces(1, b)
        for q in range(4):
            rows = slice(q * 128, (q + 1) * 128)
            out[p, rows] = (lat[b, rows].astype(F32) + whole(b, q, fx, fy)).astype(BF)
        return carry

    lax.fori_loop(0, S, hidden_one, 0)

    def finish(g, carry):
        for n in range(2):
            for c in copies(n, g):
                c.wait_send()
        return carry

    lax.fori_loop(0, GROUPS, finish, 0)


def branch(lat, g1, k1, g2, k2, owner, slot, dest):
    vm = pl.BlockSpec(memory_space=pltpu.VMEM)
    sm = pl.BlockSpec(memory_space=pltpu.SMEM)
    layer = pltpu.VMEM((S + 1, LAYER, C), BF)
    return pl.pallas_call(
        branch_kernel,
        out_shape=jax.ShapeDtypeStruct((S, CELLS, C), BF),
        in_specs=[vm, vm, vm, vm, vm, sm, sm, sm],
        out_specs=vm,
        scratch_shapes=[
            pltpu.VMEM((S + 1, CELLS, C), BF),
            pltpu.VMEM((S + 1, CELLS, C), BF),
            *([layer] * 12),
            pltpu.VMEM((S, CELLS, C), F32),
            pltpu.VMEM((2, 5, 2 * C, 2 * C), BF),
            pltpu.SemaphoreType.DMA((2, 4, GROUPS)),
            pltpu.SemaphoreType.DMA((2, 4, GROUPS)),
        ],
        compiler_params=pltpu.CompilerParams(
            collective_id=0, has_side_effects=True, vmem_limit_bytes=LIMIT
        ),
        cost_estimate=pl.CostEstimate(flops=7 * 10**9, bytes_accessed=8 * 10**6, transcendentals=6 * 10**6),
        name="branch",
    )(lat, g1, k1, g2, k2, owner, slot, dest)


def spread_kernel(hid, table, out, index, *scratch):
    came = scratch[:CHUNKS]
    ready = scratch[CHUNKS : 2 * CHUNKS]
    ys, yr, zs, zr, own = scratch[2 * CHUNKS :]
    gx = lax.axis_index("gx")
    gy = lax.axis_index("gy")
    z, y = gy // 4, gy % 4

    def along_y(d):
        return (gx, z * 4 + lax.rem(y + d, 4))

    def along_z(d):
        return (gx, lax.rem(z + d, 4) * 4 + y)

    barrier = pltpu.get_barrier_semaphore()
    for d in range(1, 4):
        pl.semaphore_signal(barrier, inc=1, device_id=along_y(d), device_id_type=MESH)
        pl.semaphore_signal(barrier, inc=1, device_id=along_z(d), device_id_type=MESH)
    pl.semaphore_wait(barrier, 6)

    def y_copy(c, d):
        rows = pl.ds(c * CR, CR)
        return pltpu.make_async_remote_copy(
            src_ref=hid.at[pl.ds(6 * d, 6), rows],
            dst_ref=came[c].at[pl.ds(6 * d, 6)],
            send_sem=ys.at[c, d],
            recv_sem=yr.at[c, d],
            device_id=along_y(d),
            device_id_type=MESH,
        )

    def z_copy(c, d):
        return pltpu.make_async_remote_copy(
            src_ref=ready[c].at[pl.ds(6 * d, 6)],
            dst_ref=out.at[pl.ds(6 * d, 6), pl.ds(c * CR, CR)],
            send_sem=zs.at[c, d],
            recv_sem=zr.at[c, d],
            device_id=along_z(d),
            device_id_type=MESH,
        )

    def own_copy(c):
        return pltpu.make_async_copy(
            ready[c].at[pl.ds(0, 6)], out.at[pl.ds(0, 6), pl.ds(c * CR, CR)], own.at[c]
        )

    for c in range(CHUNKS):
        for d in range(1, 4):
            y_copy(c, d).start()

    def count(g):
        def one(s, n):
            return n + jnp.where(table[g, s] >= 0, 1, 0)

        return lax.fori_loop(0, S, one, 0)

    def of_class(g):
        n = count(g)
        return (n - ((y - table[g, 0]) & 3) + 3) // 4, n

    here = 4 * z
    ends = []
    total = 0
    for k in range(4):
        m, _ = of_class(here + k)
        total = total + m
        ends.append(total)
    starts = [0] + ends[:3]
    z_first = 0
    for k in reversed(range(4)):
        first_slot = (y - table[here + k, 0]) & 3
        d = table[here + k, 0] + first_slot
        z_k = (d // 4) & 3
        z_first = jnp.where(ends[k] - starts[k] > 0, z_k, z_first)

    def pick(p):
        q = ((z + p // 6 - z_first) & 3) + 4 * (p % 6)
        q = jnp.minimum(q, jnp.maximum(total - 1, 0))
        k = jnp.where(q >= ends[0], 1, 0) + jnp.where(q >= ends[1], 1, 0) + jnp.where(q >= ends[2], 1, 0)
        begin = jnp.where(k == 0, starts[0], jnp.where(k == 1, starts[1], jnp.where(k == 2, starts[2], starts[3])))
        return ((y - k) & 3) * 6 + jnp.minimum(q - begin, 5)

    arriving = []
    for k in range(4):
        n_all = 0
        base = 0
        for g in reversed(range(4)):
            n = count(4 * k + g)
            n_all = n_all + n
            base = jnp.where(n > 0, table[4 * k + g, 0], base)
        arriving.append((n_all - ((gy - base) & 15) + 15) // 16)

    def index_one(t, carry):
        at, begin = S, 0
        for k in range(4):
            inside = (t >= begin) & (t < begin + arriving[k])
            at = jnp.where(inside, ((z - k) & 3) * 6 + t - begin, at)
            begin = begin + arriving[k]
        index[t] = at
        return carry

    lax.fori_loop(0, S, index_one, 0)

    for c in range(CHUNKS):
        came[c][0:6] = hid[0:6, c * CR : (c + 1) * CR]
        for d in range(1, 4):
            y_copy(c, d).wait_recv()

        def gather(p, carry):
            ready[c][p] = came[c][pick(p)]
            return carry

        lax.fori_loop(0, S, gather, 0)
        for d in range(1, 4):
            z_copy(c, d).start()
        own_copy(c).start()
    for c in range(CHUNKS):
        own_copy(c).wait()
        for d in range(1, 4):
            y_copy(c, d).wait_send()
            z_copy(c, d).wait_send()
            z_copy(c, d).wait_recv()


def spread(hid, table):
    part = pltpu.VMEM((S, CR, C), BF)
    return pl.pallas_call(
        spread_kernel,
        out_shape=(
            jax.ShapeDtypeStruct((S, CELLS, C), BF),
            jax.ShapeDtypeStruct((S,), jnp.int32),
        ),
        in_specs=[pl.BlockSpec(memory_space=pltpu.VMEM), pl.BlockSpec(memory_space=pltpu.SMEM)],
        out_specs=(pl.BlockSpec(memory_space=pl.ANY), pl.BlockSpec(memory_space=pltpu.SMEM)),
        scratch_shapes=[
            *([part] * (2 * CHUNKS)),
            *([pltpu.SemaphoreType.DMA((CHUNKS, 4))] * 4),
            pltpu.SemaphoreType.DMA((CHUNKS,)),
        ],
        compiler_params=pltpu.CompilerParams(
            collective_id=1, has_side_effects=True, vmem_limit_bytes=LIMIT
        ),
        name="spread",
    )(hid, table)


def raise_kernel(index, moved, up, out, wide, weights):
    t = pl.program_id(0)

    @pl.when(t == 0)
    def _():
        for o1 in range(2):
            for o2 in range(2):
                for o3 in range(2):
                    weights[o1, o3 * C : (o3 + 1) * C, o2 * C : (o2 + 1) * C] = up[o1, o2, o3]

    at = index[t]
    keep = jnp.where(at < S, 1.0, 0.0)
    parity = lax.broadcasted_iota(jnp.int32, (128, C), 0) % 2
    even = jnp.where(parity == 0, keep, 0.0).astype(BF)
    odd = jnp.where(parity == 1, keep, 0.0).astype(BF)
    for i in range(8):
        v = moved[0, i * 64 : (i + 1) * 64].astype(F32)
        wide[i, pl.ds(0, 64, stride=2)] = v
        wide[i, pl.ds(1, 64, stride=2)] = v
        twice = wide[i].astype(BF)
        lhs = jnp.concatenate([twice * even, twice * odd], 1)
        for o1 in range(2):
            r = dot(lhs, weights[o1])
            r0 = r[:, :C].reshape(2, 4, 2, 8, C)
            r1 = r[:, C:].reshape(2, 4, 2, 8, C)
            both = jnp.concatenate([r0, r1], 3).astype(BF)
            a, u = i // 4, 2 * (i % 4) + o1
            for b in range(2):
                for m in range(2):
                    out[4 * a + 2 * b + m, u * 64 : (u + 1) * 64] = both[b, :, m].reshape(64, C)


def raise_(index, moved, up):
    def block_of(t, index):
        return (jnp.minimum(index[t], S - 1), 0, 0)

    return pl.pallas_call(
        raise_kernel,
        out_shape=jax.ShapeDtypeStruct((8 * S, CELLS, C), BF),
        grid_spec=pltpu.PrefetchScalarGridSpec(
            num_scalar_prefetch=1,
            grid=(S,),
            in_specs=[
                pl.BlockSpec((1, CELLS, C), block_of),
                pl.BlockSpec((2, 2, 2, C, C), lambda t, index: (0, 0, 0, 0, 0)),
            ],
            out_specs=pl.BlockSpec((8, CELLS, C), lambda t, index: (t, 0, 0)),
            scratch_shapes=[pltpu.VMEM((8, 128, C), F32), pltpu.VMEM((2, 2 * C, 2 * C), BF)],
        ),
        compiler_params=pltpu.CompilerParams(
            dimension_semantics=("arbitrary",), vmem_limit_bytes=LIMIT
        ),
        name="raise",
    )(index, moved, up)


def per_device(
    latents, gain_first, conv_first, gain_second, conv_second, upward,
    neighbour_owner, neighbour_slot, destination_device, destination_slot,
):
    lat = latents.reshape(S, CELLS, C)
    dest = destination_device.reshape(1, S)
    table = lax.all_gather(destination_device.reshape(S), "gy")
    packed = branch(
        lat, gain_first.reshape(1, C), conv_first, gain_second.reshape(1, C), conv_second,
        neighbour_owner.reshape(S, 6), neighbour_slot.reshape(S, 6), dest,
    )
    arrived, index = spread(packed, table)
    children = raise_(index, arrived, upward)
    return children.reshape(1, 1, 8 * S, CELLS, C)


def solution(mesh):
    placed = (
        P("gx", "gy", None, None, None),
        P(), P(), P(), P(), P(),
        P("gx", "gy", None, None),
        P("gx", "gy", None, None),
        P("gx", "gy", None),
        P("gx", "gy", None),
    )
    return jax.shard_map(
        per_device,
        mesh=mesh,
        in_specs=placed,
        out_specs=P("gx", "gy", None, None, None),
        check_vma=False,
    )
```

```python
import jax
import jax.numpy as jnp
from jax import lax
from jax.experimental import pallas as pl
from jax.experimental.pallas import tpu as pltpu
from jax.sharding import PartitionSpec as P

MESH = pl.DeviceIdType.MESH
BF = jnp.bfloat16
F32 = jnp.float32
S = 24
C = 128
CELLS = 512
LAYER = 64
GROUPS = 4
GS = S // GROUPS
CHUNKS = 8
CR = CELLS // CHUNKS
LIMIT = 60 * 2**20


def dot(a, b):
    return jnp.dot(a, b, preferred_element_type=F32)


def main_kernel(lat_hbm, g1, k1, g2, k2, owner, slot, dest, out, index, *scratch):
    (
        lat, first, second, yl1, yh1, yl2, yh2,
        ra0, ra1, ra2, ra3, rb0, rb1, rb2, rb3,
        mixed, weights, face_x, face_y, hid, tabs, tab, picks,
        lat_sem, send_sem, recv_sem, tab_send, tab_recv, tab_sem,
        ys, yr, zs, zr, own,
    ) = scratch[: -2 * CHUNKS]
    came = scratch[-2 * CHUNKS : -CHUNKS]
    ready = scratch[-CHUNKS:]
    gx = lax.axis_index("gx")
    gy = lax.axis_index("gy")
    n_gx = lax.axis_size("gx")
    n_gy = lax.axis_size("gy")
    me = gx * n_gy + gy
    z, y = gy // 4, gy % 4
    targets = (
        (lax.rem(gx + n_gx - 1, n_gx), gy),
        (lax.rem(gx + 1, n_gx), gy),
        (gx, lax.rem(gy + n_gy - 1, n_gy)),
        (gx, lax.rem(gy + 1, n_gy)),
    )

    def along_y(d):
        return (gx, z * 4 + lax.rem(y + d, 4))

    def along_z(d):
        return (gx, lax.rem(z + d, 4) * 4 + y)

    barrier = pltpu.get_barrier_semaphore()
    for t in targets:
        pl.semaphore_signal(barrier, inc=1, device_id=t, device_id_type=MESH)
    for d in range(1, 4):
        pl.semaphore_signal(barrier, inc=1, device_id=along_y(d), device_id_type=MESH)
        pl.semaphore_signal(barrier, inc=1, device_id=along_z(d), device_id_type=MESH)

    def fetch(g):
        part = pl.ds(g * GS, GS)
        return pltpu.make_async_copy(lat_hbm.at[part], lat.at[part], lat_sem.at[g])

    for g in range(GROUPS):
        fetch(g).start()

    zero = jnp.zeros((LAYER, C), BF)
    for buf in (yl1, yh1, yl2, yh2, ra0, ra1, ra2, ra3, rb0, rb1, rb2, rb3):
        buf[S] = zero
    for buf in (first, second):
        for q in range(8):
            buf[S, q * LAYER : (q + 1) * LAYER] = zero

    recv = ((ra0, ra1, ra2, ra3), (rb0, rb1, rb2, rb3))
    acts = (first, second)
    y_lo = (yl1, yl2)
    y_hi = (yh1, yh2)
    taps = (k1, k2)

    for n in range(2):
        k = taps[n]
        o = jnp.zeros((C, C), BF)
        tiles = (
            ((k[0], k[3]), (k[1], o)),
            ((o, k[4]), (k[2], o)),
            ((k[5], o), (o, k[6])),
            ((k[1], o), (o, k[2])),
            ((k[3], o), (o, k[4])),
        )
        for w in range(5):
            for r in range(2):
                for c in range(2):
                    weights[n, w, r * C : (r + 1) * C, c * C : (c + 1) * C] = tiles[w][r][c]

    def copies(n, g):
        blocks = pl.ds(g * GS, GS)
        src = (
            acts[n].at[blocks, pl.ds(0, LAYER)],
            acts[n].at[blocks, pl.ds(CELLS - LAYER, LAYER)],
            y_lo[n].at[blocks],
            y_hi[n].at[blocks],
        )
        return [
            pltpu.make_async_remote_copy(
                src_ref=src[i],
                dst_ref=recv[n][i].at[blocks],
                send_sem=send_sem.at[n, i, g],
                recv_sem=recv_sem.at[n, i, g],
                device_id=targets[i],
                device_id_type=MESH,
            )
            for i in range(4)
        ]

    def emit(n, b, q, m, half_gain):
        scale = lax.rsqrt(jnp.mean(m * m, axis=-1, keepdims=True) + 1e-6)
        h = m * scale * half_gain
        act = h + h * jnp.tanh(h)
        acts[n][b, q * 128 : (q + 1) * 128] = act.astype(BF)
        y_lo[n][b, q * 16 : (q + 1) * 16] = jnp.concatenate([act[0:8], act[64:72]], 0).astype(BF)
        y_hi[n][b, q * 16 : (q + 1) * 16] = jnp.concatenate([act[56:64], act[120:128]], 0).astype(BF)

    def local_slot(b, f):
        s = slot[f, 0, b]
        return jnp.where((s >= 0) & (owner[f, 0, b] == me), s, S)

    def remote_slot(b, f):
        s = slot[f, 0, b]
        return jnp.where((s >= 0) & (owner[f, 0, b] != me), s, S)

    def count(s, n):
        return n + jnp.where(dest[0, s] >= 0, 1, 0)

    base = dest[0, 0]
    held = lax.fori_loop(0, S, count, 0)
    lane = lax.broadcasted_iota(jnp.int32, (8, C), 1)
    tabs[0] = jnp.where(lane == 0, held, base)

    def tab_copy(k, d):
        if k == 0:
            src, dst, to = tabs.at[0], tabs.at[d], along_y(d)
        else:
            src, dst, to = tabs.at[pl.ds(0, 4)], tabs.at[pl.ds(4 * d, 4)], along_z(d)
        return pltpu.make_async_remote_copy(
            src_ref=src,
            dst_ref=dst,
            send_sem=tab_send.at[k, d],
            recv_sem=tab_recv.at[k, d],
            device_id=to,
            device_id_type=MESH,
        )

    half_1 = g1[...] * 0.5

    def norm_group(g, carry):
        fetch(g).wait()

        def one(b, carry):
            for q in range(4):
                emit(0, b, q, lat[b, q * 128 : (q + 1) * 128].astype(F32), half_1)
            return carry

        lax.fori_loop(0, GS, lambda t, k: one(g * GS + t, k), 0, unroll=2)
        for c in copies(0, g):
            c.start()
        return carry

    pl.semaphore_wait(barrier, 10)
    for d in range(1, 4):
        tab_copy(0, d).start()
    lax.fori_loop(0, GROUPS, norm_group, 0)
    for d in range(1, 4):
        tab_copy(0, d).wait()
    for d in range(1, 4):
        tab_copy(1, d).start()

    row = lax.broadcasted_iota(jnp.int32, (128, C), 0) % 8
    low = jnp.where(row == 0, 1.0, 0.0).astype(BF)
    not_low = jnp.where(row == 0, 0.0, 1.0).astype(BF)
    high = jnp.where(row == 7, 1.0, 0.0).astype(BF)
    not_high = jnp.where(row == 7, 0.0, 1.0).astype(BF)

    def inner(n, b):
        v = acts[n]
        up = local_slot(b, 4)
        down = local_slot(b, 5)
        zero8 = jnp.zeros((8, C), F32)
        for q in range(4):
            lo, hi = q * 128, (q + 1) * 128
            here = v[b, lo:hi]
            after = v[b, lo + 64 : hi + 64] if q < 3 else jnp.concatenate([v[b, lo + 64 : hi], zero], 0)
            before = v[b, lo - 64 : hi - 64] if q > 0 else jnp.concatenate([zero, v[b, lo : hi - 64]], 0)
            a = dot(jnp.concatenate([here, after], 1), weights[n, 0])
            p = dot(jnp.concatenate([here, before], 1), weights[n, 1])
            z_up = here * not_low + v[up, lo:hi] * low
            z_down = here * not_high + v[down, lo:hi] * high
            w = dot(jnp.concatenate([z_up, z_down], 1), weights[n, 2])
            total = a[:, :C] + p[:, :C]
            total += pltpu.roll(w[:, :C].reshape(16, 8, C), 7, 1).reshape(128, C)
            total += pltpu.roll(w[:, C:].reshape(16, 8, C), 1, 1).reshape(128, C)
            yp, ym = a[:, C:], p[:, C:]
            total += jnp.concatenate([yp[8:64], zero8, yp[72:128], zero8], 0)
            total += jnp.concatenate([zero8, ym[0:56], zero8, ym[64:120]], 0)
            mixed[b, lo:hi] = total

    def faces(n, b):
        v, r = acts[n], recv[n]
        x_pair = jnp.concatenate(
            [
                v[local_slot(b, 0), 0:LAYER] + r[0][remote_slot(b, 0)],
                v[local_slot(b, 1), CELLS - LAYER : CELLS] + r[1][remote_slot(b, 1)],
            ],
            1,
        )
        y_pair = jnp.concatenate(
            [
                y_lo[n][local_slot(b, 2)] + r[2][remote_slot(b, 2)],
                y_hi[n][local_slot(b, 3)] + r[3][remote_slot(b, 3)],
            ],
            1,
        )
        return dot(x_pair, weights[n, 3]), dot(y_pair, weights[n, 4])

    def plane(b, i, fx, fy):
        m = mixed[b, i * 64 : (i + 1) * 64]
        if i == 0:
            m = m + fx[:, C:]
        if i == 7:
            m = m + fx[:, :C]
        return jnp.concatenate([m[0:8] + fy[:, C:], m[8:56], m[56:64] + fy[:, :C]], 0)

    def run_inner(n):
        def one(b, carry):
            inner(n, b)
            return carry

        lax.fori_loop(0, S, one, 0, unroll=2)

    def wait_faces(n):
        def one(g, carry):
            for c in copies(n, g):
                c.wait_recv()
            return carry

        lax.fori_loop(0, GROUPS, one, 0)

    run_inner(0)
    wait_faces(0)

    half_2 = g2[...] * 0.5

    def second_group(g, carry):
        def one(b, carry):
            fx, fy = faces(0, b)
            for q in range(4):
                both = [plane(b, i, fx, fy[8 * i : 8 * i + 8]) for i in (2 * q, 2 * q + 1)]
                emit(1, b, q, jnp.concatenate(both, 0), half_2)
            return carry

        lax.fori_loop(0, GS, lambda t, k: one(g * GS + t, k), 0, unroll=3)
        for c in copies(1, g):
            c.start()
        return carry

    lax.fori_loop(0, GROUPS, second_group, 0)
    run_inner(1)

    def source_of(p):
        return ((y + p // 6 - base) & 3) + 4 * (p % 6)

    wait_faces(1)

    def face_one(p, carry):
        fx, fy = faces(1, source_of(p))
        face_x[p] = fx
        face_y[p] = fy
        return carry

    lax.fori_loop(0, S, face_one, 0, unroll=8)

    def y_copy(c, d):
        return pltpu.make_async_remote_copy(
            src_ref=hid.at[pl.ds(6 * d, 6), pl.ds(c * CR, CR)],
            dst_ref=came[c].at[pl.ds(6 * d, 6)],
            send_sem=ys.at[c, d],
            recv_sem=yr.at[c, d],
            device_id=along_y(d),
            device_id_type=MESH,
        )

    def z_copy(c, d):
        return pltpu.make_async_remote_copy(
            src_ref=ready[c].at[pl.ds(6 * d, 6)],
            dst_ref=out.at[pl.ds(6 * d, 6), pl.ds(c * CR, CR)],
            send_sem=zs.at[c, d],
            recv_sem=zr.at[c, d],
            device_id=along_z(d),
            device_id_type=MESH,
        )

    def own_copy(c):
        return pltpu.make_async_copy(
            ready[c].at[pl.ds(0, 6)], out.at[pl.ds(0, 6), pl.ds(c * CR, CR)], own.at[c]
        )

    planes = CR // 64
    for c in range(CHUNKS):

        def rows_of(p, j):
            i = planes * c + j
            b = source_of(p)
            whole = plane(b, i, face_x[p] if i in (0, 7) else None, face_y[p, 8 * i : 8 * i + 8])
            return (lat[b, i * 64 : (i + 1) * 64].astype(F32) + whole).astype(BF)

        def sent(p, carry):
            for j in range(planes):
                i = planes * c + j
                hid[p, i * 64 : (i + 1) * 64] = rows_of(p, j)
            return carry

        def kept(p, carry):
            for j in range(planes):
                came[c][p, j * 64 : (j + 1) * 64] = rows_of(p, j)
            return carry

        lax.fori_loop(6, S, sent, 0, unroll=6)
        for d in range(1, 4):
            y_copy(c, d).start()
        lax.fori_loop(0, 6, kept, 0, unroll=6)

    for d in range(1, 4):
        tab_copy(1, d).wait()
    tab_local = pltpu.make_async_copy(tabs, tab, tab_sem)
    tab_local.start()
    tab_local.wait()

    def held_by(kz, ky):
        at = ((z - kz) & 3) * 4 + ((y - ky) & 3)
        return tab[at, 0, 0], tab[at, 0, 1]

    ends = []
    total = 0
    z_first = 0
    for k in reversed(range(4)):
        n, b0 = held_by(z, k)
        offset = (y - b0) & 3
        z_first = jnp.where(n > offset, ((b0 + offset) // 4) & 3, z_first)
    for k in range(4):
        n, b0 = held_by(z, k)
        total = total + (n - ((y - b0) & 3) + 3) // 4
        ends.append(total)
    starts = [0] + ends[:3]

    def pick(p):
        q = ((z + p // 6 - z_first) & 3) + 4 * (p % 6)
        q = jnp.minimum(q, jnp.maximum(total - 1, 0))
        k = jnp.where(q >= ends[0], 1, 0) + jnp.where(q >= ends[1], 1, 0) + jnp.where(q >= ends[2], 1, 0)
        begin = jnp.where(k == 0, starts[0], jnp.where(k == 1, starts[1], jnp.where(k == 2, starts[2], starts[3])))
        return ((y - k) & 3) * 6 + jnp.minimum(q - begin, 5)

    arriving = []
    for k in range(4):
        n_all = 0
        b_all = 0
        for j in reversed(range(4)):
            n, b0 = held_by(k, j)
            n_all = n_all + n
            b_all = jnp.where(n > 0, b0, b_all)
        arriving.append((n_all - ((gy - b_all) & 15) + 15) // 16)

    def index_one(t, carry):
        at, begin = S, 0
        for k in range(4):
            inside = (t >= begin) & (t < begin + arriving[k])
            at = jnp.where(inside, ((z - k) & 3) * 6 + t - begin, at)
            begin = begin + arriving[k]
        index[t] = at
        return carry

    lax.fori_loop(0, S, index_one, 0)

    def pick_one(p, carry):
        picks[p] = pick(p)
        return carry

    lax.fori_loop(0, S, pick_one, 0)

    for c in range(CHUNKS):
        for d in range(1, 4):
            y_copy(c, d).wait_recv()

        def gather(p, carry):
            ready[c][p] = came[c][picks[p]]
            return carry

        lax.fori_loop(0, S, gather, 0, unroll=4)
        for d in range(1, 4):
            z_copy(c, d).start()
        own_copy(c).start()

    def finish(g, carry):
        for n in range(2):
            for c in copies(n, g):
                c.wait_send()
        return carry

    lax.fori_loop(0, GROUPS, finish, 0)
    for c in range(CHUNKS):
        own_copy(c).wait()
        for d in range(1, 4):
            y_copy(c, d).wait_send()
            z_copy(c, d).wait_send()
            z_copy(c, d).wait_recv()


def main(lat, g1, k1, g2, k2, owner, slot, dest):
    vm = pl.BlockSpec(memory_space=pltpu.VMEM)
    sm = pl.BlockSpec(memory_space=pltpu.SMEM)
    anywhere = pl.BlockSpec(memory_space=pl.ANY)
    layer = pltpu.VMEM((S + 1, LAYER, C), BF)
    dma = pltpu.SemaphoreType.DMA
    return pl.pallas_call(
        main_kernel,
        out_shape=(
            jax.ShapeDtypeStruct((S, CELLS, C), BF),
            jax.ShapeDtypeStruct((S,), jnp.int32),
        ),
        in_specs=[anywhere, vm, vm, vm, vm, sm, sm, sm],
        out_specs=(anywhere, sm),
        scratch_shapes=[
            pltpu.VMEM((S, CELLS, C), BF),
            pltpu.VMEM((S + 1, CELLS, C), BF),
            pltpu.VMEM((S + 1, CELLS, C), BF),
            *([layer] * 12),
            pltpu.VMEM((S, CELLS, C), F32),
            pltpu.VMEM((2, 5, 2 * C, 2 * C), BF),
            pltpu.VMEM((S, LAYER, 2 * C), F32),
            pltpu.VMEM((S, LAYER, 2 * C), F32),
            pltpu.VMEM((S, CELLS, C), BF),
            pltpu.VMEM((16, 8, C), jnp.int32),
            pltpu.SMEM((16, 8, C), jnp.int32),
            pltpu.SMEM((S,), jnp.int32),
            dma((GROUPS,)),
            dma((2, 4, GROUPS)),
            dma((2, 4, GROUPS)),
            dma((2, 4)),
            dma((2, 4)),
            dma,
            *([dma((CHUNKS, 4))] * 4),
            dma((CHUNKS,)),
            *([pltpu.VMEM((S, CR, C), BF)] * (2 * CHUNKS)),
        ],
        compiler_params=pltpu.CompilerParams(
            collective_id=0, has_side_effects=True, vmem_limit_bytes=LIMIT
        ),
        cost_estimate=pl.CostEstimate(flops=7 * 10**9, bytes_accessed=8 * 10**6, transcendentals=6 * 10**6),
        name="main",
    )(lat, g1, k1, g2, k2, owner, slot, dest)


DEPTH = 4


def raise_kernel(index, moved, up, out, blocks, even, odd, weights, done, in_sem, out_sem):
    def get(t):
        return pltpu.make_async_copy(moved.at[jnp.minimum(index[t], S - 1)], blocks.at[t], in_sem.at[t])

    def put(t):
        return pltpu.make_async_copy(done.at[t % DEPTH], out.at[pl.ds(8 * t, 8)], out_sem.at[t % DEPTH])

    def fetch(t, carry):
        get(t).start()
        return carry

    lax.fori_loop(0, S, fetch, 0)
    for o1 in range(2):
        for o2 in range(2):
            for o3 in range(2):
                weights[o1, o3 * C : (o3 + 1) * C, o2 * C : (o2 + 1) * C] = up[o1, o2, o3]
    even[...] = jnp.zeros_like(even)
    odd[...] = jnp.zeros_like(odd)

    def step(t, carry):
        get(t).wait()

        @pl.when(t >= DEPTH)
        def _():
            put(t - DEPTH).wait()

        keep = index[t] < S
        for i in range(8):
            v = blocks[t, i * 64 : (i + 1) * 64].astype(F32)
            v = jnp.where(keep, v, 0.0)
            even[i, pl.ds(0, 64, stride=2)] = v
            odd[i, pl.ds(1, 64, stride=2)] = v
        for o1 in range(2):
            for h in range(2):
                rows = slice(4 * h, 4 * h + 4)
                lhs = jnp.concatenate(
                    [even[rows].reshape(512, C).astype(BF), odd[rows].reshape(512, C).astype(BF)], 1
                )
                r = dot(lhs, weights[o1])
                for k in range(4):
                    part = r[k * 128 : (k + 1) * 128]
                    r0 = part[:, :C].reshape(2, 4, 2, 8, C)
                    r1 = part[:, C:].reshape(2, 4, 2, 8, C)
                    both = jnp.concatenate([r0, r1], 3).astype(BF)
                    u = 2 * k + o1
                    for b in range(2):
                        for m in range(2):
                            done[t % DEPTH, 4 * h + 2 * b + m, u * 64 : (u + 1) * 64] = both[
                                b, :, m
                            ].reshape(64, C)
        put(t).start()
        return carry

    lax.fori_loop(0, S, step, 0)

    def finish(t, carry):
        put(t).wait()
        return carry

    lax.fori_loop(S - DEPTH, S, finish, 0)


def raise_(index, moved, up):
    return pl.pallas_call(
        raise_kernel,
        out_shape=jax.ShapeDtypeStruct((8 * S, CELLS, C), BF),
        in_specs=[
            pl.BlockSpec(memory_space=pltpu.SMEM),
            pl.BlockSpec(memory_space=pl.ANY),
            pl.BlockSpec(memory_space=pltpu.VMEM),
        ],
        out_specs=pl.BlockSpec(memory_space=pl.ANY),
        scratch_shapes=[
            pltpu.VMEM((S, CELLS, C), BF),
            pltpu.VMEM((8, 128, C), F32),
            pltpu.VMEM((8, 128, C), F32),
            pltpu.VMEM((2, 2 * C, 2 * C), BF),
            pltpu.VMEM((DEPTH, 8, CELLS, C), BF),
            pltpu.SemaphoreType.DMA((S,)),
            pltpu.SemaphoreType.DMA((DEPTH,)),
        ],
        compiler_params=pltpu.CompilerParams(vmem_limit_bytes=LIMIT),
        name="raise",
    )(index, moved, up)


def per_device(
    latents, gain_first, conv_first, gain_second, conv_second, upward,
    neighbour_owner, neighbour_slot, destination_device, destination_slot,
):
    arrived, index = main(
        latents.reshape(S, CELLS, C),
        gain_first.reshape(1, C),
        conv_first,
        gain_second.reshape(1, C),
        conv_second,
        neighbour_owner.reshape(S, 6).T.reshape(6, 1, S),
        neighbour_slot.reshape(S, 6).T.reshape(6, 1, S),
        destination_device.reshape(1, S),
    )
    children = raise_(index, arrived, upward)
    return children.reshape(1, 1, 8 * S, CELLS, C)


def solution(mesh):
    placed = (
        P("gx", "gy", None, None, None),
        P(), P(), P(), P(), P(),
        P("gx", "gy", None, None),
        P("gx", "gy", None, None),
        P("gx", "gy", None),
        P("gx", "gy", None),
    )
    return jax.shard_map(
        per_device,
        mesh=mesh,
        in_specs=placed,
        out_specs=P("gx", "gy", None, None, None),
        check_vma=False,
    )
```

```python
import jax
import jax.numpy as jnp
from jax import lax
from jax.experimental import pallas as pl
from jax.experimental.pallas import tpu as pltpu
from jax.sharding import PartitionSpec as P

MESH = pl.DeviceIdType.MESH
BF = jnp.bfloat16
F32 = jnp.float32
S = 24
C = 128
CELLS = 512
LAYER = 64
GROUPS = 4
GS = S // GROUPS
CHUNKS = 16
CR = CELLS // CHUNKS
LIMIT = 60 * 2**20


def dot(a, b):
    return jnp.dot(a, b, preferred_element_type=F32)


def main_kernel(lat_hbm, g1, k1_hbm, g2, k2_hbm, owner, slot, dest, out, index, *scratch):
    (
        lat, k1, k2, first, second, yl1, yh1, yl2, yh2,
        ra0, ra1, ra2, ra3, rb0, rb1, rb2, rb3,
        mixed, weights, face_x, face_y, hid, tabs, tab, picks,
        lat_sem, tap_sem, send_sem, recv_sem, tab_send, tab_recv, tab_sem,
        ys, yr, zs, zr, own,
    ) = scratch[: -2 * CHUNKS]
    came = scratch[-2 * CHUNKS : -CHUNKS]
    ready = scratch[-CHUNKS:]
    gx = lax.axis_index("gx")
    gy = lax.axis_index("gy")
    n_gx = lax.axis_size("gx")
    n_gy = lax.axis_size("gy")
    me = gx * n_gy + gy
    z, y = gy // 4, gy % 4
    targets = (
        (lax.rem(gx + n_gx - 1, n_gx), gy),
        (lax.rem(gx + 1, n_gx), gy),
        (gx, lax.rem(gy + n_gy - 1, n_gy)),
        (gx, lax.rem(gy + 1, n_gy)),
    )

    def along_y(d):
        return (gx, z * 4 + lax.rem(y + d, 4))

    def along_z(d):
        return (gx, lax.rem(z + d, 4) * 4 + y)

    barrier = pltpu.get_barrier_semaphore()
    for t in targets:
        pl.semaphore_signal(barrier, inc=1, device_id=t, device_id_type=MESH)
    for d in range(1, 4):
        pl.semaphore_signal(barrier, inc=1, device_id=along_y(d), device_id_type=MESH)
        pl.semaphore_signal(barrier, inc=1, device_id=along_z(d), device_id_type=MESH)

    def fetch(g):
        part = pl.ds(g * GS, GS)
        return pltpu.make_async_copy(lat_hbm.at[part], lat.at[part], lat_sem.at[g])

    for g in range(GROUPS):
        fetch(g).start()
    fetch_taps = (
        pltpu.make_async_copy(k1_hbm, k1, tap_sem.at[0]),
        pltpu.make_async_copy(k2_hbm, k2, tap_sem.at[1]),
    )
    for c in fetch_taps:
        c.start()

    recv = ((ra0, ra1, ra2, ra3), (rb0, rb1, rb2, rb3))
    acts = (first, second)
    y_lo = (yl1, yl2)
    y_hi = (yh1, yh2)
    taps = (k1, k2)

    def copies(n, g):
        blocks = pl.ds(g * GS, GS)
        src = (
            acts[n].at[blocks, pl.ds(0, LAYER)],
            acts[n].at[blocks, pl.ds(CELLS - LAYER, LAYER)],
            y_lo[n].at[blocks],
            y_hi[n].at[blocks],
        )
        return [
            pltpu.make_async_remote_copy(
                src_ref=src[i],
                dst_ref=recv[n][i].at[blocks],
                send_sem=send_sem.at[n, i, g],
                recv_sem=recv_sem.at[n, i, g],
                device_id=targets[i],
                device_id_type=MESH,
            )
            for i in range(4)
        ]

    def strip(ref, b, first_row):
        return jnp.concatenate([ref[b, 64 * i + first_row : 64 * i + first_row + 16] for i in range(8)], 0)

    def emit(n, b, s, m, half_gain):
        scale = lax.rsqrt(jnp.mean(m * m, axis=-1, keepdims=True) + 1e-6)
        h = m * scale * half_gain
        act = h + h * jnp.tanh(h)
        rounded = act.astype(BF)
        for i in range(8):
            acts[n][b, 64 * i + 16 * s : 64 * i + 16 * s + 16] = rounded[16 * i : 16 * i + 16]
        if s == 0:
            y_lo[n][b] = jnp.concatenate([act[16 * i : 16 * i + 8] for i in range(8)], 0).astype(BF)
        if s == 3:
            y_hi[n][b] = jnp.concatenate([act[16 * i + 8 : 16 * i + 16] for i in range(8)], 0).astype(BF)

    def local_slot(b, f):
        s = slot[f, 0, b]
        return jnp.where((s >= 0) & (owner[f, 0, b] == me), s, S)

    def remote_slot(b, f):
        s = slot[f, 0, b]
        return jnp.where((s >= 0) & (owner[f, 0, b] != me), s, S)

    def count(s, n):
        return n + jnp.where(dest[0, s] >= 0, 1, 0)

    base = dest[0, 0]
    held = lax.fori_loop(0, S, count, 0)
    lane = lax.broadcasted_iota(jnp.int32, (8, C), 1)
    tabs[0] = jnp.where(lane == 0, held, base)

    def tab_copy(k, d):
        if k == 0:
            src, dst, to = tabs.at[0], tabs.at[d], along_y(d)
        else:
            src, dst, to = tabs.at[pl.ds(0, 4)], tabs.at[pl.ds(4 * d, 4)], along_z(d)
        return pltpu.make_async_remote_copy(
            src_ref=src,
            dst_ref=dst,
            send_sem=tab_send.at[k, d],
            recv_sem=tab_recv.at[k, d],
            device_id=to,
            device_id_type=MESH,
        )

    half_1 = g1[...] * 0.5

    def norm_group(g):
        fetch(g).wait()

        def one(b, carry):
            for s in range(4):
                emit(0, b, s, strip(lat, b, 16 * s).astype(F32), half_1)
            return carry

        lax.fori_loop(0, GS, lambda t, k: one(g * GS + t, k), 0, unroll=2)

    def norm_and_send(g, carry):
        norm_group(g)
        for c in copies(0, g):
            c.start()
        return carry

    norm_group(0)
    pl.semaphore_wait(barrier, 10)
    for c in copies(0, 0):
        c.start()
    for d in range(1, 4):
        tab_copy(0, d).start()
    lax.fori_loop(1, GROUPS, norm_and_send, 0)

    zero = jnp.zeros((LAYER, C), BF)
    for buf in (yl1, yh1, yl2, yh2, ra0, ra1, ra2, ra3, rb0, rb1, rb2, rb3):
        buf[S] = zero
    for buf in (first, second):
        for q in range(8):
            buf[S, q * LAYER : (q + 1) * LAYER] = zero

    for c in fetch_taps:
        c.wait()
    for n in range(2):
        k = taps[n]
        o = jnp.zeros((C, C), BF)
        tiles = (
            ((k[0], k[1]), (k[3], o)),
            ((o, k[2]), (k[4], o)),
            ((k[5], o), (o, k[6])),
            ((k[1], o), (o, k[2])),
            ((k[3], o), (o, k[4])),
        )
        for w in range(5):
            for r in range(2):
                for c in range(2):
                    weights[n, w, r * C : (r + 1) * C, c * C : (c + 1) * C] = tiles[w][r][c]

    for d in range(1, 4):
        tab_copy(0, d).wait()
    for d in range(1, 4):
        tab_copy(1, d).start()

    row = lax.broadcasted_iota(jnp.int32, (128, C), 0) % 8
    low = jnp.where(row == 0, 1.0, 0.0).astype(BF)
    not_low = jnp.where(row == 0, 0.0, 1.0).astype(BF)
    high = jnp.where(row == 7, 1.0, 0.0).astype(BF)
    not_high = jnp.where(row == 7, 0.0, 1.0).astype(BF)

    def inner(n, b, s):
        v = acts[n]
        up = local_slot(b, 4)
        down = local_slot(b, 5)
        zero8 = jnp.zeros((8, C), BF)
        zero16 = jnp.zeros((16, C), F32)
        here = strip(v, b, 16 * s)
        if s < 3:
            after = strip(v, b, 16 * s + 8)
        else:
            after = jnp.concatenate([x for i in range(8) for x in (v[b, 64 * i + 56 : 64 * i + 64], zero8)], 0)
        if s > 0:
            before = strip(v, b, 16 * s - 8)
        else:
            before = jnp.concatenate([x for i in range(8) for x in (zero8, v[b, 64 * i : 64 * i + 8])], 0)
        a = dot(jnp.concatenate([here, after], 1), weights[n, 0])
        p = dot(jnp.concatenate([here, before], 1), weights[n, 1])
        z_up = here * not_low + strip(v, up, 16 * s) * low
        z_down = here * not_high + strip(v, down, 16 * s) * high
        w = dot(jnp.concatenate([z_up, z_down], 1), weights[n, 2])
        total = a[:, :C] + p[:, :C]
        total += pltpu.roll(w[:, :C].reshape(16, 8, C), 7, 1).reshape(128, C)
        total += pltpu.roll(w[:, C:].reshape(16, 8, C), 1, 1).reshape(128, C)
        total += jnp.concatenate([a[16:, C:], zero16], 0)
        total += jnp.concatenate([zero16, p[:112, C:]], 0)
        mixed[b, 128 * s : 128 * s + 128] = total

    def x_faces(n, b):
        v, r = acts[n], recv[n]
        pair = jnp.concatenate(
            [
                v[local_slot(b, 0), 0:LAYER] + r[0][remote_slot(b, 0)],
                v[local_slot(b, 1), CELLS - LAYER : CELLS] + r[1][remote_slot(b, 1)],
            ],
            1,
        )
        return dot(pair, weights[n, 3])

    def y_faces(n, b):
        r = recv[n]
        pair = jnp.concatenate(
            [
                y_lo[n][local_slot(b, 2)] + r[2][remote_slot(b, 2)],
                y_hi[n][local_slot(b, 3)] + r[3][remote_slot(b, 3)],
            ],
            1,
        )
        return dot(pair, weights[n, 4])

    def whole(b, s, fx, fy):
        m = mixed[b, 128 * s : 128 * s + 128]
        pieces = []
        for i in range(8):
            even, odd = m[16 * i : 16 * i + 8], m[16 * i + 8 : 16 * i + 16]
            if i in (0, 7):
                lanes = slice(C, 2 * C) if i == 0 else slice(0, C)
                even = even + fx[16 * s : 16 * s + 8, lanes]
                odd = odd + fx[16 * s + 8 : 16 * s + 16, lanes]
            if s == 0:
                even = even + fy[8 * i : 8 * i + 8, C:]
            if s == 3:
                odd = odd + fy[8 * i : 8 * i + 8, :C]
            pieces += [even, odd]
        return jnp.concatenate(pieces, 0)

    def run_inner(n, strips):
        def one(b, carry):
            for s in strips:
                inner(n, b, s)
            return carry

        lax.fori_loop(0, S, one, 0, unroll=12 // len(strips))

    def wait_faces(n, which):
        def one(g, carry):
            for c in copies(n, g)[which]:
                c.wait_recv()
            return carry

        lax.fori_loop(0, GROUPS, one, 0)

    run_inner(0, (0, 1, 2, 3))
    wait_faces(0, slice(0, 4))

    half_2 = g2[...] * 0.5

    def second_group(g, carry):
        def one(b, carry):
            fx, fy = x_faces(0, b), y_faces(0, b)
            for s in range(4):
                emit(1, b, s, whole(b, s, fx, fy), half_2)
            return carry

        lax.fori_loop(0, GS, lambda t, k: one(g * GS + t, k), 0, unroll=3)
        for c in copies(1, g):
            c.start()
        return carry

    lax.fori_loop(0, GROUPS, second_group, 0)

    def source_of(p):
        return ((y + p // 6 - base) & 3) + 4 * (p % 6)

    def x_one(p, carry):
        face_x[p] = x_faces(1, source_of(p))
        return carry

    def y_one(p, carry):
        face_y[p] = y_faces(1, source_of(p))
        return carry

    def y_copy(c, d):
        return pltpu.make_async_remote_copy(
            src_ref=hid.at[pl.ds(6 * d, 6), pl.ds(c * CR, CR)],
            dst_ref=came[c].at[pl.ds(6 * d, 6)],
            send_sem=ys.at[c, d],
            recv_sem=yr.at[c, d],
            device_id=along_y(d),
            device_id_type=MESH,
        )

    def z_copy(c, d):
        return pltpu.make_async_remote_copy(
            src_ref=ready[c].at[pl.ds(6 * d, 6)],
            dst_ref=out.at[pl.ds(6 * d, 6), pl.ds(c * CR, CR)],
            send_sem=zs.at[c, d],
            recv_sem=zr.at[c, d],
            device_id=along_z(d),
            device_id_type=MESH,
        )

    def own_copy(c):
        return pltpu.make_async_copy(
            ready[c].at[pl.ds(0, 6)], out.at[pl.ds(0, 6), pl.ds(c * CR, CR)], own.at[c]
        )

    parts = 128 // CR

    def hidden(s):
        def rows_of(p):
            b = source_of(p)
            branch = whole(b, s, face_x[p], face_y[p] if s in (0, 3) else None)
            return (strip(lat, b, 16 * s).astype(F32) + branch).astype(BF)

        def sent(p, carry):
            hid[p, s * 128 : (s + 1) * 128] = rows_of(p)
            return carry

        def kept(p, carry):
            rows = rows_of(p)
            for j in range(parts):
                came[parts * s + j][p] = rows[j * CR : (j + 1) * CR]
            return carry

        lax.fori_loop(6, S, sent, 0, unroll=3)
        for c in range(parts * s, parts * (s + 1)):
            for d in range(1, 4):
                y_copy(c, d).start()
        lax.fori_loop(0, 6, kept, 0, unroll=3)

    run_inner(1, (1, 2))
    wait_faces(1, slice(0, 2))
    lax.fori_loop(0, S, x_one, 0, unroll=8)
    hidden(1)
    hidden(2)

    for d in range(1, 4):
        tab_copy(1, d).wait()
    tab_local = pltpu.make_async_copy(tabs, tab, tab_sem)
    tab_local.start()
    tab_local.wait()

    def held_by(kz, ky):
        at = ((z - kz) & 3) * 4 + ((y - ky) & 3)
        return tab[at, 0, 0], tab[at, 0, 1]

    ends = []
    total = 0
    z_first = 0
    for k in reversed(range(4)):
        n, b0 = held_by(z, k)
        offset = (y - b0) & 3
        z_first = jnp.where(n > offset, ((b0 + offset) // 4) & 3, z_first)
    for k in range(4):
        n, b0 = held_by(z, k)
        total = total + (n - ((y - b0) & 3) + 3) // 4
        ends.append(total)
    starts = [0] + ends[:3]

    def pick(p):
        q = ((z + p // 6 - z_first) & 3) + 4 * (p % 6)
        q = jnp.minimum(q, jnp.maximum(total - 1, 0))
        k = jnp.where(q >= ends[0], 1, 0) + jnp.where(q >= ends[1], 1, 0) + jnp.where(q >= ends[2], 1, 0)
        begin = jnp.where(k == 0, starts[0], jnp.where(k == 1, starts[1], jnp.where(k == 2, starts[2], starts[3])))
        return ((y - k) & 3) * 6 + jnp.minimum(q - begin, 5)

    arriving = []
    for k in range(4):
        n_all = 0
        b_all = 0
        for j in reversed(range(4)):
            n, b0 = held_by(k, j)
            n_all = n_all + n
            b_all = jnp.where(n > 0, b0, b_all)
        arriving.append((n_all - ((gy - b_all) & 15) + 15) // 16)

    def index_one(t, carry):
        at, begin = S, 0
        for k in range(4):
            inside = (t >= begin) & (t < begin + arriving[k])
            at = jnp.where(inside, ((z - k) & 3) * 6 + t - begin, at)
            begin = begin + arriving[k]
        index[t] = at
        return carry

    lax.fori_loop(0, S, index_one, 0)

    def pick_one(p, carry):
        picks[p] = pick(p)
        return carry

    lax.fori_loop(0, S, pick_one, 0)

    def relay(c):
        for d in range(1, 4):
            y_copy(c, d).wait_recv()

        def gather(p, carry):
            ready[c][p] = came[c][picks[p]]
            return carry

        lax.fori_loop(0, S, gather, 0, unroll=4)
        for d in range(1, 4):
            z_copy(c, d).start()
        own_copy(c).start()

    order = [parts * s + j for s in (1, 2, 0, 3) for j in range(parts)]
    run_inner(1, (0, 3))
    for c in order[:1]:
        relay(c)
    wait_faces(1, slice(2, 4))
    lax.fori_loop(0, S, y_one, 0, unroll=8)
    hidden(0)
    for c in order[1:2]:
        relay(c)
    hidden(3)
    for c in order[2:]:
        relay(c)

    def finish(g, carry):
        for n in range(2):
            for c in copies(n, g):
                c.wait_send()
        return carry

    lax.fori_loop(0, GROUPS, finish, 0)
    for c in range(CHUNKS):
        own_copy(c).wait()
        for d in range(1, 4):
            y_copy(c, d).wait_send()
            z_copy(c, d).wait_send()
            z_copy(c, d).wait_recv()


def main(lat, g1, k1, g2, k2, owner, slot, dest):
    vm = pl.BlockSpec(memory_space=pltpu.VMEM)
    sm = pl.BlockSpec(memory_space=pltpu.SMEM)
    anywhere = pl.BlockSpec(memory_space=pl.ANY)
    layer = pltpu.VMEM((S + 1, LAYER, C), BF)
    dma = pltpu.SemaphoreType.DMA
    return pl.pallas_call(
        main_kernel,
        out_shape=(
            jax.ShapeDtypeStruct((S, CELLS, C), BF),
            jax.ShapeDtypeStruct((S,), jnp.int32),
        ),
        in_specs=[anywhere, vm, anywhere, vm, anywhere, sm, sm, sm],
        out_specs=(anywhere, sm),
        scratch_shapes=[
            pltpu.VMEM((S, CELLS, C), BF),
            pltpu.VMEM((7, C, C), BF),
            pltpu.VMEM((7, C, C), BF),
            pltpu.VMEM((S + 1, CELLS, C), BF),
            pltpu.VMEM((S + 1, CELLS, C), BF),
            *([layer] * 12),
            pltpu.VMEM((S, CELLS, C), F32),
            pltpu.VMEM((2, 5, 2 * C, 2 * C), BF),
            pltpu.VMEM((S, LAYER, 2 * C), F32),
            pltpu.VMEM((S, LAYER, 2 * C), F32),
            pltpu.VMEM((S, CELLS, C), BF),
            pltpu.VMEM((16, 8, C), jnp.int32),
            pltpu.SMEM((16, 8, C), jnp.int32),
            pltpu.SMEM((S,), jnp.int32),
            dma((GROUPS,)),
            dma((2,)),
            dma((2, 4, GROUPS)),
            dma((2, 4, GROUPS)),
            dma((2, 4)),
            dma((2, 4)),
            dma,
            *([dma((CHUNKS, 4))] * 4),
            dma((CHUNKS,)),
            *([pltpu.VMEM((S, CR, C), BF)] * (2 * CHUNKS)),
        ],
        compiler_params=pltpu.CompilerParams(
            collective_id=0, has_side_effects=True, vmem_limit_bytes=LIMIT
        ),
        cost_estimate=pl.CostEstimate(flops=7 * 10**9, bytes_accessed=8 * 10**6, transcendentals=6 * 10**6),
        name="main",
    )(lat, g1, k1, g2, k2, owner, slot, dest)


DEPTH = 4


def raise_kernel(index, moved, up, out, blocks, even, odd, weights, done, in_sem, out_sem):
    def get(t):
        return pltpu.make_async_copy(moved.at[jnp.minimum(index[t], S - 1)], blocks.at[t], in_sem.at[t])

    def put(t):
        return pltpu.make_async_copy(done.at[t % DEPTH], out.at[pl.ds(8 * t, 8)], out_sem.at[t % DEPTH])

    def fetch(t, carry):
        get(t).start()
        return carry

    lax.fori_loop(0, S, fetch, 0)
    for o1 in range(2):
        for o2 in range(2):
            for o3 in range(2):
                weights[o1, o3 * C : (o3 + 1) * C, o2 * C : (o2 + 1) * C] = up[o1, o2, o3]
    even[...] = jnp.zeros_like(even)
    odd[...] = jnp.zeros_like(odd)

    def step(t, carry):
        get(t).wait()

        @pl.when(t >= DEPTH)
        def _():
            put(t - DEPTH).wait()

        keep = index[t] < S
        for i in range(8):
            v = jnp.concatenate(
                [blocks[t, 128 * s + 16 * i : 128 * s + 16 * i + 16] for s in range(4)], 0
            ).astype(F32)
            v = jnp.where(keep, v, 0.0)
            even[i, pl.ds(0, 64, stride=2)] = v
            odd[i, pl.ds(1, 64, stride=2)] = v
        for o1 in range(2):
            for h in range(2):
                rows = slice(4 * h, 4 * h + 4)
                lhs = jnp.concatenate(
                    [even[rows].reshape(512, C).astype(BF), odd[rows].reshape(512, C).astype(BF)], 1
                )
                r = dot(lhs, weights[o1])
                for k in range(4):
                    part = r[k * 128 : (k + 1) * 128]
                    r0 = part[:, :C].reshape(2, 4, 2, 8, C)
                    r1 = part[:, C:].reshape(2, 4, 2, 8, C)
                    both = jnp.concatenate([r0, r1], 3).astype(BF)
                    u = 2 * k + o1
                    for b in range(2):
                        for m in range(2):
                            done[t % DEPTH, 4 * h + 2 * b + m, u * 64 : (u + 1) * 64] = both[
                                b, :, m
                            ].reshape(64, C)
        put(t).start()
        return carry

    lax.fori_loop(0, S, step, 0)

    def finish(t, carry):
        put(t).wait()
        return carry

    lax.fori_loop(S - DEPTH, S, finish, 0)


def raise_(index, moved, up):
    return pl.pallas_call(
        raise_kernel,
        out_shape=jax.ShapeDtypeStruct((8 * S, CELLS, C), BF),
        in_specs=[
            pl.BlockSpec(memory_space=pltpu.SMEM),
            pl.BlockSpec(memory_space=pl.ANY),
            pl.BlockSpec(memory_space=pltpu.VMEM),
        ],
        out_specs=pl.BlockSpec(memory_space=pl.ANY),
        scratch_shapes=[
            pltpu.VMEM((S, CELLS, C), BF),
            pltpu.VMEM((8, 128, C), F32),
            pltpu.VMEM((8, 128, C), F32),
            pltpu.VMEM((2, 2 * C, 2 * C), BF),
            pltpu.VMEM((DEPTH, 8, CELLS, C), BF),
            pltpu.SemaphoreType.DMA((S,)),
            pltpu.SemaphoreType.DMA((DEPTH,)),
        ],
        compiler_params=pltpu.CompilerParams(vmem_limit_bytes=LIMIT),
        name="raise",
    )(index, moved, up)


def per_device(
    latents, gain_first, conv_first, gain_second, conv_second, upward,
    neighbour_owner, neighbour_slot, destination_device, destination_slot,
):
    arrived, index = main(
        latents.reshape(S, CELLS, C),
        gain_first.reshape(1, C),
        conv_first,
        gain_second.reshape(1, C),
        conv_second,
        neighbour_owner.reshape(S, 6).T.reshape(6, 1, S),
        neighbour_slot.reshape(S, 6).T.reshape(6, 1, S),
        destination_device.reshape(1, S),
    )
    children = raise_(index, arrived, upward)
    return children.reshape(1, 1, 8 * S, CELLS, C)


def solution(mesh):
    placed = (
        P("gx", "gy", None, None, None),
        P(), P(), P(), P(), P(),
        P("gx", "gy", None, None),
        P("gx", "gy", None, None),
        P("gx", "gy", None),
        P("gx", "gy", None),
    )
    return jax.shard_map(
        per_device,
        mesh=mesh,
        in_specs=placed,
        out_specs=P("gx", "gy", None, None, None),
        check_vma=False,
    )
```

```python
import jax
import jax.numpy as jnp
from jax import lax
from jax.experimental import pallas as pl
from jax.experimental.pallas import tpu as pltpu
from jax.sharding import PartitionSpec as P

MESH = pl.DeviceIdType.MESH
BF = jnp.bfloat16
F32 = jnp.float32
S = 24
C = 128
CELLS = 512
LAYER = 64
GROUPS = 4
GS = S // GROUPS
CHUNKS = 16
CR = CELLS // CHUNKS
LIMIT = 60 * 2**20


def dot(a, b):
    return jnp.dot(a, b, preferred_element_type=F32)


def main_kernel(lat_hbm, g1, k1_hbm, g2, k2_hbm, owner, slot, dest, out, index, *scratch):
    (
        lat, k1, k2, first, second, yl1, yh1, yl2, yh2,
        ra0, ra1, ra2, ra3, rb0, rb1, rb2, rb3,
        mixed, weights, face_x, face_y, hid, tabs, tab, picks,
        lat_sem, tap_sem, send_sem, recv_sem, tab_send, tab_recv, tab_sem,
        ys, yr, zs, zr, own,
    ) = scratch[: -2 * CHUNKS]
    came = scratch[-2 * CHUNKS : -CHUNKS]
    ready = scratch[-CHUNKS:]
    gx = lax.axis_index("gx")
    gy = lax.axis_index("gy")
    n_gx = lax.axis_size("gx")
    n_gy = lax.axis_size("gy")
    me = gx * n_gy + gy
    z, y = gy // 4, gy % 4
    targets = (
        (lax.rem(gx + n_gx - 1, n_gx), gy),
        (lax.rem(gx + 1, n_gx), gy),
        (gx, lax.rem(gy + n_gy - 1, n_gy)),
        (gx, lax.rem(gy + 1, n_gy)),
    )

    def along_y(d):
        return (gx, z * 4 + lax.rem(y + d, 4))

    def along_z(d):
        return (gx, lax.rem(z + d, 4) * 4 + y)

    barrier = pltpu.get_barrier_semaphore()
    for t in targets:
        pl.semaphore_signal(barrier, inc=1, device_id=t, device_id_type=MESH)
    for d in range(1, 4):
        pl.semaphore_signal(barrier, inc=1, device_id=along_y(d), device_id_type=MESH)
        pl.semaphore_signal(barrier, inc=1, device_id=along_z(d), device_id_type=MESH)

    def fetch(g):
        part = pl.ds(g * GS, GS)
        return pltpu.make_async_copy(lat_hbm.at[part], lat.at[part], lat_sem.at[g])

    for g in range(GROUPS):
        fetch(g).start()
    fetch_taps = (
        pltpu.make_async_copy(k1_hbm, k1, tap_sem.at[0]),
        pltpu.make_async_copy(k2_hbm, k2, tap_sem.at[1]),
    )
    for c in fetch_taps:
        c.start()

    recv = ((ra0, ra1, ra2, ra3), (rb0, rb1, rb2, rb3))
    acts = (first, second)
    y_lo = (yl1, yl2)
    y_hi = (yh1, yh2)
    taps = (k1, k2)

    def copies(n, g):
        blocks = pl.ds(g * GS, GS)
        src = (
            acts[n].at[blocks, pl.ds(0, LAYER)],
            acts[n].at[blocks, pl.ds(CELLS - LAYER, LAYER)],
            y_lo[n].at[blocks],
            y_hi[n].at[blocks],
        )
        return [
            pltpu.make_async_remote_copy(
                src_ref=src[i],
                dst_ref=recv[n][i].at[blocks],
                send_sem=send_sem.at[n, i, g],
                recv_sem=recv_sem.at[n, i, g],
                device_id=targets[i],
                device_id_type=MESH,
            )
            for i in range(4)
        ]

    def strip(ref, b, first_row):
        return jnp.concatenate([ref[b, 64 * i + first_row : 64 * i + first_row + 16] for i in range(8)], 0)

    def emit(n, b, s, m, half_gain):
        scale = lax.rsqrt(jnp.mean(m * m, axis=-1, keepdims=True) + 1e-6)
        h = m * scale * half_gain
        act = h + h * jnp.tanh(h)
        rounded = act.astype(BF)
        for i in range(8):
            acts[n][b, 64 * i + 16 * s : 64 * i + 16 * s + 16] = rounded[16 * i : 16 * i + 16]
        if s == 0:
            y_lo[n][b] = jnp.concatenate([act[16 * i : 16 * i + 8] for i in range(8)], 0).astype(BF)
        if s == 3:
            y_hi[n][b] = jnp.concatenate([act[16 * i + 8 : 16 * i + 16] for i in range(8)], 0).astype(BF)

    def local_slot(b, f):
        s = slot[f, 0, b]
        return jnp.where((s >= 0) & (owner[f, 0, b] == me), s, S)

    def remote_slot(b, f):
        s = slot[f, 0, b]
        return jnp.where((s >= 0) & (owner[f, 0, b] != me), s, S)

    def count(s, n):
        return n + jnp.where(dest[0, s] >= 0, 1, 0)

    base = dest[0, 0]
    held = lax.fori_loop(0, S, count, 0)
    lane = lax.broadcasted_iota(jnp.int32, (8, C), 1)
    tabs[0] = jnp.where(lane == 0, held, base)

    def tab_copy(k, d):
        if k == 0:
            src, dst, to = tabs.at[0], tabs.at[d], along_y(d)
        else:
            src, dst, to = tabs.at[pl.ds(0, 4)], tabs.at[pl.ds(4 * d, 4)], along_z(d)
        return pltpu.make_async_remote_copy(
            src_ref=src,
            dst_ref=dst,
            send_sem=tab_send.at[k, d],
            recv_sem=tab_recv.at[k, d],
            device_id=to,
            device_id_type=MESH,
        )

    half_1 = g1[...] * 0.5

    def norm_group(g):
        fetch(g).wait()

        def one(b, carry):
            for s in range(4):
                emit(0, b, s, strip(lat, b, 16 * s).astype(F32), half_1)
            return carry

        lax.fori_loop(0, GS, lambda t, k: one(g * GS + t, k), 0, unroll=3)

    def norm_and_send(g, carry):
        norm_group(g)
        for c in copies(0, g):
            c.start()
        return carry

    norm_group(0)
    pl.semaphore_wait(barrier, 10)
    for c in copies(0, 0):
        c.start()
    for d in range(1, 4):
        tab_copy(0, d).start()
    lax.fori_loop(1, GROUPS, norm_and_send, 0)

    zero = jnp.zeros((LAYER, C), BF)
    for buf in (yl1, yh1, yl2, yh2, ra0, ra1, ra2, ra3, rb0, rb1, rb2, rb3):
        buf[S] = zero
    for buf in (first, second):
        for q in range(8):
            buf[S, q * LAYER : (q + 1) * LAYER] = zero

    for c in fetch_taps:
        c.wait()
    for n in range(2):
        k = taps[n]
        o = jnp.zeros((C, C), BF)
        tiles = (
            ((k[0], k[1]), (k[3], o)),
            ((o, k[2]), (k[4], o)),
            ((k[5], o), (o, k[6])),
            ((k[1], o), (o, k[2])),
            ((k[3], o), (o, k[4])),
        )
        for w in range(5):
            for r in range(2):
                for c in range(2):
                    weights[n, w, r * C : (r + 1) * C, c * C : (c + 1) * C] = tiles[w][r][c]

    for d in range(1, 4):
        tab_copy(0, d).wait()
    for d in range(1, 4):
        tab_copy(1, d).start()

    row = lax.broadcasted_iota(jnp.int32, (128, C), 0) % 8
    low = jnp.where(row == 0, 1.0, 0.0).astype(BF)
    not_low = jnp.where(row == 0, 0.0, 1.0).astype(BF)
    high = jnp.where(row == 7, 1.0, 0.0).astype(BF)
    not_high = jnp.where(row == 7, 0.0, 1.0).astype(BF)

    def inner(n, b, s):
        v = acts[n]
        up = local_slot(b, 4)
        down = local_slot(b, 5)
        zero8 = jnp.zeros((8, C), BF)
        zero16 = jnp.zeros((16, C), F32)
        here = strip(v, b, 16 * s)
        if s < 3:
            after = strip(v, b, 16 * s + 8)
        else:
            after = jnp.concatenate([x for i in range(8) for x in (v[b, 64 * i + 56 : 64 * i + 64], zero8)], 0)
        if s > 0:
            before = strip(v, b, 16 * s - 8)
        else:
            before = jnp.concatenate([x for i in range(8) for x in (zero8, v[b, 64 * i : 64 * i + 8])], 0)
        a = dot(jnp.concatenate([here, after], 1), weights[n, 0])
        p = dot(jnp.concatenate([here, before], 1), weights[n, 1])
        z_up = here * not_low + strip(v, up, 16 * s) * low
        z_down = here * not_high + strip(v, down, 16 * s) * high
        w = dot(jnp.concatenate([z_up, z_down], 1), weights[n, 2])
        total = a[:, :C] + p[:, :C]
        total += pltpu.roll(w[:, :C].reshape(16, 8, C), 7, 1).reshape(128, C)
        total += pltpu.roll(w[:, C:].reshape(16, 8, C), 1, 1).reshape(128, C)
        total += jnp.concatenate([a[16:, C:], zero16], 0)
        total += jnp.concatenate([zero16, p[:112, C:]], 0)
        mixed[b, 128 * s : 128 * s + 128] = total

    def x_faces(n, b):
        v, r = acts[n], recv[n]
        pair = jnp.concatenate(
            [
                v[local_slot(b, 0), 0:LAYER] + r[0][remote_slot(b, 0)],
                v[local_slot(b, 1), CELLS - LAYER : CELLS] + r[1][remote_slot(b, 1)],
            ],
            1,
        )
        return dot(pair, weights[n, 3])

    def y_faces(n, b):
        r = recv[n]
        pair = jnp.concatenate(
            [
                y_lo[n][local_slot(b, 2)] + r[2][remote_slot(b, 2)],
                y_hi[n][local_slot(b, 3)] + r[3][remote_slot(b, 3)],
            ],
            1,
        )
        return dot(pair, weights[n, 4])

    def whole(b, s, fx, fy):
        m = mixed[b, 128 * s : 128 * s + 128]
        pieces = []
        for i in range(8):
            even, odd = m[16 * i : 16 * i + 8], m[16 * i + 8 : 16 * i + 16]
            if i in (0, 7):
                lanes = slice(C, 2 * C) if i == 0 else slice(0, C)
                even = even + fx[16 * s : 16 * s + 8, lanes]
                odd = odd + fx[16 * s + 8 : 16 * s + 16, lanes]
            if s == 0:
                even = even + fy[8 * i : 8 * i + 8, C:]
            if s == 3:
                odd = odd + fy[8 * i : 8 * i + 8, :C]
            pieces += [even, odd]
        return jnp.concatenate(pieces, 0)

    def run_inner(n, strips):
        def one(b, carry):
            for s in strips:
                inner(n, b, s)
            return carry

        lax.fori_loop(0, S, one, 0, unroll=12 // len(strips))

    def wait_faces(n, which):
        def one(g, carry):
            for c in copies(n, g)[which]:
                c.wait_recv()
            return carry

        lax.fori_loop(0, GROUPS, one, 0)

    run_inner(0, (0, 1, 2, 3))
    wait_faces(0, slice(0, 4))

    half_2 = g2[...] * 0.5

    def second_group(g, carry):
        def one(b, carry):
            fx, fy = x_faces(0, b), y_faces(0, b)
            for s in range(4):
                emit(1, b, s, whole(b, s, fx, fy), half_2)
            return carry

        lax.fori_loop(0, GS, lambda t, k: one(g * GS + t, k), 0, unroll=6)
        for c in copies(1, g):
            c.start()
        return carry

    lax.fori_loop(0, GROUPS, second_group, 0)

    def source_of(p):
        return ((y + p // 6 - base) & 3) + 4 * (p % 6)

    def x_one(p, carry):
        face_x[p] = x_faces(1, source_of(p))
        return carry

    def y_one(p, carry):
        face_y[p] = y_faces(1, source_of(p))
        return carry

    def y_copy(c, d):
        return pltpu.make_async_remote_copy(
            src_ref=hid.at[pl.ds(6 * d, 6), pl.ds(c * CR, CR)],
            dst_ref=came[c].at[pl.ds(6 * d, 6)],
            send_sem=ys.at[c, d],
            recv_sem=yr.at[c, d],
            device_id=along_y(d),
            device_id_type=MESH,
        )

    def z_copy(c, d):
        return pltpu.make_async_remote_copy(
            src_ref=ready[c].at[pl.ds(6 * d, 6)],
            dst_ref=out.at[pl.ds(6 * d, 6), pl.ds(c * CR, CR)],
            send_sem=zs.at[c, d],
            recv_sem=zr.at[c, d],
            device_id=along_z(d),
            device_id_type=MESH,
        )

    def own_copy(c):
        return pltpu.make_async_copy(
            ready[c].at[pl.ds(0, 6)], out.at[pl.ds(0, 6), pl.ds(c * CR, CR)], own.at[c]
        )

    parts = 128 // CR

    def hidden(s):
        def rows_of(p):
            b = source_of(p)
            branch = whole(b, s, face_x[p], face_y[p] if s in (0, 3) else None)
            return (strip(lat, b, 16 * s).astype(F32) + branch).astype(BF)

        def sent(p, carry):
            hid[p, s * 128 : (s + 1) * 128] = rows_of(p)
            return carry

        def kept(p, carry):
            rows = rows_of(p)
            for j in range(parts):
                came[parts * s + j][p] = rows[j * CR : (j + 1) * CR]
            return carry

        lax.fori_loop(6, S, sent, 0, unroll=6)
        for c in range(parts * s, parts * (s + 1)):
            for d in range(1, 4):
                y_copy(c, d).start()
        lax.fori_loop(0, 6, kept, 0, unroll=6)

    run_inner(1, (1, 2))
    wait_faces(1, slice(0, 2))
    lax.fori_loop(0, S, x_one, 0, unroll=8)
    hidden(1)
    hidden(2)

    for d in range(1, 4):
        tab_copy(1, d).wait()
    tab_local = pltpu.make_async_copy(tabs, tab, tab_sem)
    tab_local.start()
    tab_local.wait()

    def held_by(kz, ky):
        at = ((z - kz) & 3) * 4 + ((y - ky) & 3)
        return tab[at, 0, 0], tab[at, 0, 1]

    ends = []
    total = 0
    z_first = 0
    for k in reversed(range(4)):
        n, b0 = held_by(z, k)
        offset = (y - b0) & 3
        z_first = jnp.where(n > offset, ((b0 + offset) // 4) & 3, z_first)
    for k in range(4):
        n, b0 = held_by(z, k)
        total = total + (n - ((y - b0) & 3) + 3) // 4
        ends.append(total)
    starts = [0] + ends[:3]

    def pick(p):
        q = ((z + p // 6 - z_first) & 3) + 4 * (p % 6)
        q = jnp.minimum(q, jnp.maximum(total - 1, 0))
        k = jnp.where(q >= ends[0], 1, 0) + jnp.where(q >= ends[1], 1, 0) + jnp.where(q >= ends[2], 1, 0)
        begin = jnp.where(k == 0, starts[0], jnp.where(k == 1, starts[1], jnp.where(k == 2, starts[2], starts[3])))
        return ((y - k) & 3) * 6 + jnp.minimum(q - begin, 5)

    arriving = []
    for k in range(4):
        n_all = 0
        b_all = 0
        for j in reversed(range(4)):
            n, b0 = held_by(k, j)
            n_all = n_all + n
            b_all = jnp.where(n > 0, b0, b_all)
        arriving.append((n_all - ((gy - b_all) & 15) + 15) // 16)

    def index_one(t, carry):
        at, begin = S, 0
        for k in range(4):
            inside = (t >= begin) & (t < begin + arriving[k])
            at = jnp.where(inside, ((z - k) & 3) * 6 + t - begin, at)
            begin = begin + arriving[k]
        index[t] = at
        return carry

    lax.fori_loop(0, S, index_one, 0)

    def pick_one(p, carry):
        picks[p] = pick(p)
        return carry

    lax.fori_loop(0, S, pick_one, 0)

    def relay(c):
        for d in range(1, 4):
            y_copy(c, d).wait_recv()

        def gather(p, carry):
            ready[c][p] = came[c][picks[p]]
            return carry

        lax.fori_loop(0, S, gather, 0, unroll=8)
        for d in range(1, 4):
            z_copy(c, d).start()
        own_copy(c).start()

    order = [parts * s + j for s in (1, 2, 0, 3) for j in range(parts)]
    run_inner(1, (0,))
    relay(order[0])
    run_inner(1, (3,))
    relay(order[1])
    wait_faces(1, slice(2, 4))
    lax.fori_loop(0, S, y_one, 0, unroll=8)
    hidden(0)
    relay(order[2])
    hidden(3)
    for c in order[3:]:
        relay(c)

    def finish(g, carry):
        for n in range(2):
            for c in copies(n, g):
                c.wait_send()
        return carry

    lax.fori_loop(0, GROUPS, finish, 0)
    for c in range(CHUNKS):
        own_copy(c).wait()
        for d in range(1, 4):
            y_copy(c, d).wait_send()
            z_copy(c, d).wait_send()
            z_copy(c, d).wait_recv()


def main(lat, g1, k1, g2, k2, owner, slot, dest):
    vm = pl.BlockSpec(memory_space=pltpu.VMEM)
    sm = pl.BlockSpec(memory_space=pltpu.SMEM)
    anywhere = pl.BlockSpec(memory_space=pl.ANY)
    layer = pltpu.VMEM((S + 1, LAYER, C), BF)
    dma = pltpu.SemaphoreType.DMA
    return pl.pallas_call(
        main_kernel,
        out_shape=(
            jax.ShapeDtypeStruct((S, CELLS, C), BF),
            jax.ShapeDtypeStruct((S,), jnp.int32),
        ),
        in_specs=[anywhere, vm, anywhere, vm, anywhere, sm, sm, sm],
        out_specs=(anywhere, sm),
        scratch_shapes=[
            pltpu.VMEM((S, CELLS, C), BF),
            pltpu.VMEM((7, C, C), BF),
            pltpu.VMEM((7, C, C), BF),
            pltpu.VMEM((S + 1, CELLS, C), BF),
            pltpu.VMEM((S + 1, CELLS, C), BF),
            *([layer] * 12),
            pltpu.VMEM((S, CELLS, C), F32),
            pltpu.VMEM((2, 5, 2 * C, 2 * C), BF),
            pltpu.VMEM((S, LAYER, 2 * C), F32),
            pltpu.VMEM((S, LAYER, 2 * C), F32),
            pltpu.VMEM((S, CELLS, C), BF),
            pltpu.VMEM((16, 8, C), jnp.int32),
            pltpu.SMEM((16, 8, C), jnp.int32),
            pltpu.SMEM((S,), jnp.int32),
            dma((GROUPS,)),
            dma((2,)),
            dma((2, 4, GROUPS)),
            dma((2, 4, GROUPS)),
            dma((2, 4)),
            dma((2, 4)),
            dma,
            *([dma((CHUNKS, 4))] * 4),
            dma((CHUNKS,)),
            *([pltpu.VMEM((S, CR, C), BF)] * (2 * CHUNKS)),
        ],
        compiler_params=pltpu.CompilerParams(
            collective_id=0, has_side_effects=True, vmem_limit_bytes=LIMIT
        ),
        cost_estimate=pl.CostEstimate(flops=7 * 10**9, bytes_accessed=8 * 10**6, transcendentals=6 * 10**6),
        name="main",
    )(lat, g1, k1, g2, k2, owner, slot, dest)


DEPTH = 4


def raise_kernel(index, moved, up, out, blocks, even, odd, weights, done, in_sem, out_sem):
    def get(t):
        return pltpu.make_async_copy(moved.at[jnp.minimum(index[t], S - 1)], blocks.at[t], in_sem.at[t])

    def put(t):
        return pltpu.make_async_copy(done.at[t % DEPTH], out.at[pl.ds(8 * t, 8)], out_sem.at[t % DEPTH])

    def fetch(t, carry):
        get(t).start()
        return carry

    lax.fori_loop(0, S, fetch, 0)
    for o1 in range(2):
        for o2 in range(2):
            for o3 in range(2):
                weights[o1, o3 * C : (o3 + 1) * C, o2 * C : (o2 + 1) * C] = up[o1, o2, o3]
    even[...] = jnp.zeros_like(even)
    odd[...] = jnp.zeros_like(odd)

    def step(t, carry):
        get(t).wait()

        @pl.when(t >= DEPTH)
        def _():
            put(t - DEPTH).wait()

        keep = index[t] < S
        for i in range(8):
            v = jnp.concatenate(
                [blocks[t, 128 * s + 16 * i : 128 * s + 16 * i + 16] for s in range(4)], 0
            ).astype(F32)
            v = jnp.where(keep, v, 0.0)
            even[i, pl.ds(0, 64, stride=2)] = v
            odd[i, pl.ds(1, 64, stride=2)] = v
        for o1 in range(2):
            for h in range(2):
                rows = slice(4 * h, 4 * h + 4)
                lhs = jnp.concatenate(
                    [even[rows].reshape(512, C).astype(BF), odd[rows].reshape(512, C).astype(BF)], 1
                )
                r = dot(lhs, weights[o1])
                for k in range(4):
                    part = r[k * 128 : (k + 1) * 128]
                    r0 = part[:, :C].reshape(2, 4, 2, 8, C)
                    r1 = part[:, C:].reshape(2, 4, 2, 8, C)
                    both = jnp.concatenate([r0, r1], 3).astype(BF)
                    u = 2 * k + o1
                    for b in range(2):
                        for m in range(2):
                            done[t % DEPTH, 4 * h + 2 * b + m, u * 64 : (u + 1) * 64] = both[
                                b, :, m
                            ].reshape(64, C)
        put(t).start()
        return carry

    lax.fori_loop(0, S, step, 0)

    def finish(t, carry):
        put(t).wait()
        return carry

    lax.fori_loop(S - DEPTH, S, finish, 0)


def raise_(index, moved, up):
    return pl.pallas_call(
        raise_kernel,
        out_shape=jax.ShapeDtypeStruct((8 * S, CELLS, C), BF),
        in_specs=[
            pl.BlockSpec(memory_space=pltpu.SMEM),
            pl.BlockSpec(memory_space=pl.ANY),
            pl.BlockSpec(memory_space=pltpu.VMEM),
        ],
        out_specs=pl.BlockSpec(memory_space=pl.ANY),
        scratch_shapes=[
            pltpu.VMEM((S, CELLS, C), BF),
            pltpu.VMEM((8, 128, C), F32),
            pltpu.VMEM((8, 128, C), F32),
            pltpu.VMEM((2, 2 * C, 2 * C), BF),
            pltpu.VMEM((DEPTH, 8, CELLS, C), BF),
            pltpu.SemaphoreType.DMA((S,)),
            pltpu.SemaphoreType.DMA((DEPTH,)),
        ],
        compiler_params=pltpu.CompilerParams(vmem_limit_bytes=LIMIT),
        name="raise",
    )(index, moved, up)


def per_device(
    latents, gain_first, conv_first, gain_second, conv_second, upward,
    neighbour_owner, neighbour_slot, destination_device, destination_slot,
):
    arrived, index = main(
        latents.reshape(S, CELLS, C),
        gain_first.reshape(1, C),
        conv_first,
        gain_second.reshape(1, C),
        conv_second,
        neighbour_owner.reshape(S, 6).T.reshape(6, 1, S),
        neighbour_slot.reshape(S, 6).T.reshape(6, 1, S),
        destination_device.reshape(1, S),
    )
    children = raise_(index, arrived, upward)
    return children.reshape(1, 1, 8 * S, CELLS, C)


def solution(mesh):
    placed = (
        P("gx", "gy", None, None, None),
        P(), P(), P(), P(), P(),
        P("gx", "gy", None, None),
        P("gx", "gy", None, None),
        P("gx", "gy", None),
        P("gx", "gy", None),
    )
    return jax.shard_map(
        per_device,
        mesh=mesh,
        in_specs=placed,
        out_specs=P("gx", "gy", None, None, None),
        check_vma=False,
    )
```
